32 devices in a mesh: fronts: 4 (over y, core), rows: 8 (over z, x).
Axes of the slice: x: 2, y: 2, z: 4, core: 2. Of those that a mesh axis runs over, the one named last changes fastest.
Arguments:
- lower_rhs: float32 [8, 8192, 512], P('fronts', 'rows'), may hold values from -6 to 6
- lower_vectors: float32 [8, 8192, 256], P('fronts', 'rows')
- lower_factors: float32 [8, 8, 256, 256], P('fronts', 'rows')
- merge_vectors: float32 [8, 8, 256, 256], P('fronts', 'rows')
- merge_factors: float32 [8, 8, 256, 256], P('fronts', 'rows')
- live_blocks: int32 [8], replicated, may hold values from 1 to 8, 32 in all
- parent_front: int32 [8, 1], replicated, may hold values from 0 to 3, as said below
- front_owner: int32 [4], replicated, may hold values from 0 to 3, as said below
- contrib_rows: int32 [8, 128], replicated, may hold values from 0 to 8191, as said below
- upper_rhs: float32 [4, 8192, 512], P('fronts', 'rows'), may hold values from -6 to 6
- upper_vectors: float32 [4, 8192, 256], P('fronts', 'rows')
- upper_factors: float32 [4, 8, 256, 256], P('fronts', 'rows')
- summit_vectors: float32 [4, 8, 256, 256], P('fronts', 'rows')
- summit_factors: float32 [4, 8, 256, 256], P('fronts', 'rows')
Outputs:
- lower_result: float32 [8, 8192, 512], P('fronts', 'rows')
- upper_result: float32 [4, 8192, 512], P('fronts', 'rows')
The draws below stay inside these ranges and needn't reach their ends.
Inputs may be any that keep to these rules, and one draw needn't show every extreme that they name: `parent_front`: every parent front has between one and 4 children, and some parent has exactly 4. `front_owner`: each parent front has its own index of fronts. `contrib_rows`: row k of a child's contribution lands in its parent's row block k // 16; no two entries are equal.
All inputs are finite; a program needn't handle non-finite values.
Results may differ from the reference program's by a relative error of at most 0.0003.
Values sent between devices are 32-bit elements; how exact they have to be, the bound alone decides.
A program may use at most 128 MiB of HBM per device.

```python
import math
import jax
import jax.numpy as jnp
import numpy as np
from jax import lax

N = 512
BR = 1024
K = 256
NPIV = 128
FR1 = 2
MAXCH = 4
CB = 128
CONTRIB_PER_BLOCK = 16
LOWER_FRONTS = 8
F2 = 4
FROWS = 8192
LEVELS = 3
N_ROWS = 8


def compact_factor(vectors):
    gram_matrix = jnp.einsum('cri,crj->cij', vectors, vectors, precision=lax.Precision.HIGHEST)
    unit_matrix = jnp.eye(gram_matrix.shape[-1], dtype=jnp.float32)
    triangle = jnp.triu(gram_matrix, 1) + 0.5 * gram_matrix * unit_matrix
    identity_stack = jnp.broadcast_to(unit_matrix, gram_matrix.shape)
    return jax.scipy.linalg.solve_triangular(triangle, identity_stack, lower=False)


def block_reflectors(key, number):
    normal = jax.random.normal(key, (number, BR, K), jnp.float32)
    spread = 1.0 / BR ** 0.5
    row_index = lax.broadcasted_iota(jnp.int32, (BR, K), 0)
    column_index = lax.broadcasted_iota(jnp.int32, (BR, K), 1)
    vectors = jnp.where(row_index > column_index, spread * normal, jnp.where(row_index == column_index, 1.0, 0.0))
    return (vectors, compact_factor(vectors))


def node_reflectors(key, number):
    normal = jax.random.normal(key, (number, K, K), jnp.float32)
    spread = (2.0 / K) ** 0.5
    upper_part = jnp.triu(spread * normal)
    unit_stack = jnp.broadcast_to(jnp.eye(K, dtype=jnp.float32), upper_part.shape)
    return (upper_part, compact_factor(jnp.concatenate([unit_stack, upper_part], axis=1)))


def draw_lower_vectors(key, part):
    vectors, factors = block_reflectors(jax.random.fold_in(key, 11), LOWER_FRONTS * N_ROWS)
    return vectors.reshape(LOWER_FRONTS, FROWS, K)


def draw_lower_factors(key, part):
    vectors, factors = block_reflectors(jax.random.fold_in(key, 11), LOWER_FRONTS * N_ROWS)
    return factors.reshape(LOWER_FRONTS, N_ROWS, K, K)


def draw_merge_vectors(key, part):
    vectors, factors = node_reflectors(jax.random.fold_in(key, 12), LOWER_FRONTS * N_ROWS)
    return vectors.reshape(LOWER_FRONTS, N_ROWS, K, K)


def draw_merge_factors(key, part):
    vectors, factors = node_reflectors(jax.random.fold_in(key, 12), LOWER_FRONTS * N_ROWS)
    return factors.reshape(LOWER_FRONTS, N_ROWS, K, K)


def draw_upper_vectors(key, part):
    vectors, factors = block_reflectors(jax.random.fold_in(key, 13), F2 * N_ROWS)
    return vectors.reshape(F2, FROWS, K)


def draw_upper_factors(key, part):
    vectors, factors = block_reflectors(jax.random.fold_in(key, 13), F2 * N_ROWS)
    return factors.reshape(F2, N_ROWS, K, K)


def draw_summit_vectors(key, part):
    vectors, factors = node_reflectors(jax.random.fold_in(key, 14), F2 * N_ROWS)
    return vectors.reshape(F2, N_ROWS, K, K)


def draw_summit_factors(key, part):
    vectors, factors = node_reflectors(jax.random.fold_in(key, 14), F2 * N_ROWS)
    return factors.reshape(F2, N_ROWS, K, K)


def ownership(key):
    base_key = jax.random.fold_in(key, 21)
    held = jax.random.permutation(jax.random.fold_in(base_key, 1), F2).astype(jnp.int32)
    owner = jnp.argsort(held).astype(jnp.int32)
    shuffled = jax.random.permutation(jax.random.fold_in(base_key, 2), F2).astype(jnp.int32)
    child_index = jnp.arange(LOWER_FRONTS, dtype=jnp.int32)
    device = child_index // FR1
    slot_index = child_index % FR1
    next_parent = held[(device + F2 // 2) % F2]
    picked = jnp.clip(device - (MAXCH - 2), 0, F2 - 1)
    crowd_parent = jnp.where(device < MAXCH - 1, shuffled[0], shuffled[picked])
    parent = jnp.where(slot_index == FR1 - 1, next_parent, crowd_parent)
    return (parent.astype(jnp.int32), owner)


def draw_parent_front(key, part):
    parent, owner = ownership(key)
    return parent.reshape(LOWER_FRONTS, 1)


def draw_front_owner(key, part):
    parent, owner = ownership(key)
    return owner


def block_offsets(key):
    selected_count = LOWER_FRONTS * CONTRIB_PER_BLOCK
    others = jax.random.permutation(jax.random.fold_in(key, 1), BR - 2)[:selected_count - 2] + 1
    chosen = jnp.concatenate([jnp.array([0, BR - 1], jnp.int32), others.astype(jnp.int32)])
    return jax.random.permutation(jax.random.fold_in(key, 2), chosen)


def draw_contrib_rows(key, part):
    block_keys = jax.random.split(jax.random.fold_in(key, 15), N_ROWS)
    row_offsets = jax.vmap(block_offsets)(block_keys)
    begin_positions = (jnp.arange(N_ROWS, dtype=jnp.int32) * BR)[:, None]
    positioned_rows = (row_offsets + begin_positions).reshape(N_ROWS, LOWER_FRONTS, CONTRIB_PER_BLOCK)
    return jnp.transpose(positioned_rows, (1, 0, 2)).reshape(LOWER_FRONTS, CB).astype(jnp.int32)


def steps_of(own_key, shape, cuts, least, top_value):
    gain = 1.0
    for position, shards_of in cuts:
        heights = jax.random.uniform(jax.random.fold_in(jax.random.fold_in(own_key, 6), position), (shards_of,), jnp.float32, least / len(cuts), top_value / len(cuts))
        gain = gain * jnp.repeat(jnp.exp(heights), shape[position] // shards_of).reshape((-1,) + (1,) * (len(shape) - 1 - position))
    return gain


def length_profile(count, total, bound, skew):
    portions = [(1 << 20) // math.isqrt(grade ** skew) + 1 for grade in range(2, count + 1)]
    spare, given = total - bound - (count - 1), [1] * (count - 1)
    while spare > 0:
        movable = [i for i in range(count - 1) if given[i] < bound]
        whole, left = sum([portions[i] for i in movable]), spare
        for i in movable:
            extra = min(bound - given[i], max(1, left * portions[i] // whole), spare)
            given[i] = given[i] + extra
            spare = spare - extra
    return np.array([bound] + given)


def uneven_parts(stream_key, count, total, reach, lean):
    if count == 2:
        one = jax.random.randint(stream_key, (), max(1, total - reach), min(reach, total - 1) + 1)
        return jnp.stack([one, total - one])
    sizes = jnp.asarray(length_profile(count, total, reach, lean), jnp.int32)
    twos = (count - 1) // 2
    giver, taker = sizes[1:1 + 2 * twos:2], sizes[2:2 + 2 * twos:2]
    slack = jnp.minimum(giver - 1, reach - taker)
    passed = jax.random.randint(jax.random.fold_in(stream_key, 1), (twos,), 0, 1 << 20) % (slack + 1)
    sizes = sizes.at[1:1 + 2 * twos:2].set(giver - passed).at[2:2 + 2 * twos:2].set(taker + passed)
    return sizes[jax.random.permutation(jax.random.fold_in(stream_key, 2), count)]


def gaussian(key, dims, scale, most, cuts=(), kind=jnp.bfloat16):
    values = scale * jax.random.normal(key, dims, jnp.float32)
    if cuts:
        values = values * steps_of(key, dims, cuts, -0.22, 0.18)
    return jnp.clip(values, -most, most).astype(kind)


def setup_inputs(seed: int = 0) -> dict:
    key_list = jax.random.split(jax.random.key(seed), 15)
    return {
        "lower_rhs": gaussian(key_list[0], (LOWER_FRONTS, FROWS, N), 1.0, 6.0, ((0, 4), (1, 8)), jnp.float32),
        "lower_vectors": draw_lower_vectors(jax.random.fold_in(key_list[14], 71), 0),
        "lower_factors": draw_lower_factors(jax.random.fold_in(key_list[14], 71), 0),
        "merge_vectors": draw_merge_vectors(jax.random.fold_in(key_list[14], 71), 0),
        "merge_factors": draw_merge_factors(jax.random.fold_in(key_list[14], 71), 0),
        "live_blocks": uneven_parts(key_list[5], LOWER_FRONTS, LOWER_FRONTS * N_ROWS // 2, N_ROWS, 2).astype(jnp.int32),
        "parent_front": draw_parent_front(jax.random.fold_in(key_list[14], 71), 0),
        "front_owner": draw_front_owner(jax.random.fold_in(key_list[14], 71), 0),
        "contrib_rows": draw_contrib_rows(jax.random.fold_in(key_list[14], 71), 0),
        "upper_rhs": gaussian(key_list[9], (F2, FROWS, N), 1.0, 6.0, ((0, 4), (1, 8)), jnp.float32),
        "upper_vectors": draw_upper_vectors(jax.random.fold_in(key_list[14], 71), 0),
        "upper_factors": draw_upper_factors(jax.random.fold_in(key_list[14], 71), 0),
        "summit_vectors": draw_summit_vectors(jax.random.fold_in(key_list[14], 71), 0),
        "summit_factors": draw_summit_factors(jax.random.fold_in(key_list[14], 71), 0),
    }


EXACT = lax.Precision.HIGHEST

def contract(form, left, right):
    return jnp.einsum(form, left, right, precision=EXACT)

def apply_front(values, vectors, factors, pair_vectors, pair_factors, live):
    values = values.reshape(N_ROWS, BR, -1)
    vectors = vectors.reshape(N_ROWS, BR, K)
    project = contract('fri,frn->fin', vectors, values)
    scaled = contract('fij,fin->fjn', factors, project)
    applied = values - contract('fri,fin->frn', vectors, scaled)
    index = jnp.arange(N_ROWS, dtype=jnp.int32)
    applied = jnp.where((index < live)[:, None, None], applied, values)
    tops = applied[:, :K]
    for level in range(LEVELS):
        step = 2 ** level
        lead = tops[0::2 * step]
        rest = tops[step::2 * step]
        node_vec = pair_vectors[step::2 * step]
        node_fac = pair_factors[step::2 * step]
        inner = lead + contract('fij,fin->fjn', node_vec, rest)
        weight = contract('fij,fin->fjn', node_fac, inner)
        new_lead = lead - weight
        new_rest = rest - contract('fij,fjn->fin', node_vec, weight)
        active = (index[step::2 * step] < live)[:, None, None]
        tops = tops.at[0::2 * step].set(jnp.where(active, new_lead, lead))
        tops = tops.at[step::2 * step].set(jnp.where(active, new_rest, rest))
    return (tops, applied)

def reference(lower_rhs, lower_vectors, lower_factors, merge_vectors, merge_factors, live_blocks, parent_front, front_owner, contrib_rows, upper_rhs, upper_vectors, upper_factors, summit_vectors, summit_factors):

    def lower_one(operands):
        values, vectors, factors, pair_vectors, pair_factors, live = operands
        tops, applied = apply_front(values, vectors, factors, pair_vectors, pair_factors, live)
        keep = jnp.arange(K, dtype=jnp.int32) < NPIV
        root = jnp.where(keep[:, None], tops[0], jnp.zeros_like(tops[0]))
        shown = tops.at[0].set(root)
        result = jnp.concatenate([shown, applied[:, K:]], axis=1).reshape(FROWS, -1)
        return (result, tops[0, NPIV:])
    lower_result, contrib = lax.map(lower_one, (lower_rhs, lower_vectors, lower_factors, merge_vectors, merge_factors, live_blocks))
    target = front_owner[parent_front[:, 0]]
    assembled = upper_rhs.at[target[:, None], contrib_rows].set(contrib)

    def upper_one(operands):
        values, vectors, factors, pair_vectors, pair_factors = operands
        tops, applied = apply_front(values, vectors, factors, pair_vectors, pair_factors, jnp.int32(N_ROWS))
        return jnp.concatenate([tops, applied[:, K:]], axis=1).reshape(FROWS, -1)
    upper_result = lax.map(upper_one, (assembled, upper_vectors, upper_factors, summit_vectors, summit_factors))
    return (lower_result, upper_result)
```

```python
import jax
import jax.numpy as jnp
from jax import lax
from jax.sharding import PartitionSpec as P

NPIV = 128


EXACT = lax.Precision.HIGHEST
NEAR = lax.Precision.HIGH


def moved(value, axis, pairs):
    return lax.ppermute(value, axis, pairs)


def product(form, left, right):
    return jnp.einsum(form, left, right, precision=NEAR)


def wy_apply(values, vectors, factors):
    project = product("ri,rn->in", vectors, values)
    scaled = product("ij,in->jn", factors, project)
    return values - product("ri,in->rn", vectors, scaled)


def node_pairs(axis, level):
    step = 1 << level
    return [(p, p - step) for p in range(step, lax.axis_size(axis), 2 * step)]


def lead_factors(factors, levels):
    return [moved(factors, "rows", node_pairs("rows", level)) for level in range(levels)]


def run_tree(top, vectors, leads, live, place):
    back = jnp.zeros_like(top)
    for level, factors in enumerate(leads):
        step = 1 << level
        up = node_pairs("rows", level)
        arrived = moved(product("ij,in->jn", vectors, top), "rows", up)
        weight = product("ij,in->jn", factors, top + arrived)
        active = (place % (2 * step) == 0) & (place + step < live)
        weight = jnp.where(active, weight, 0.0)
        top = top - weight
        back = back + moved(weight, "rows", [(q, p) for p, q in up])
    return top, back


def spread(contrib, place, blocks):
    piece = contrib
    step = blocks // 2
    while step:
        half = piece.shape[0] // 2
        got = moved(piece[half:], "rows", [(q, q + step) for q in range(0, blocks, 2 * step)])
        piece = jnp.where(place % (2 * step) == step, got, piece[:half])
        step //= 2
    return piece


def per_device(
    lower_rhs,
    lower_vectors,
    lower_factors,
    merge_vectors,
    merge_factors,
    live_blocks,
    parent_front,
    front_owner,
    contrib_rows,
    upper_rhs,
    upper_vectors,
    upper_factors,
    summit_vectors,
    summit_factors,
):
    place = lax.axis_index("rows")
    column = lax.axis_index("fronts")
    blocks = lax.axis_size("rows")
    local_fronts = lower_rhs.shape[0]
    height = lower_rhs.shape[1]
    width = lower_factors.shape[-1]
    live = lax.dynamic_slice_in_dim(live_blocks, column * local_fronts, local_fronts)
    levels = blocks.bit_length() - 1
    share = (width - NPIV) // blocks
    leads = [lead_factors(merge_factors[f, 0], levels) for f in range(local_fronts)]
    summit_leads = lead_factors(summit_factors[0, 0], levels)
    applied, trees, portions = [], [], []
    for f in range(local_fronts):
        done = wy_apply(lower_rhs[f], lower_vectors[f], lower_factors[f, 0])
        applied.append(jnp.where(place < live[f], done, lower_rhs[f]))
    for f in range(local_fronts):
        trees.append(
            run_tree(applied[f][:width], merge_vectors[f, 0], leads[f], live[f], place)
        )
        portions.append(spread(trees[f][0][NPIV:], place, blocks))
    mine = jnp.stack(portions)
    columns = lax.axis_size("fronts")
    gathered = jnp.zeros((columns,) + mine.shape, mine.dtype)
    gathered = lax.dynamic_update_slice_in_dim(gathered, mine[None], column, 0)
    for shift in range(1, columns):
        got = moved(mine, "fronts", [(c, (c + shift) % columns) for c in range(columns)])
        gathered = lax.dynamic_update_slice_in_dim(
            gathered, got[None], (column - shift) % columns, 0
        )
    front_portions = gathered.reshape(-1, share, gathered.shape[-1])
    parents = jnp.arange(front_owner.shape[0], dtype=jnp.int32)
    target = jnp.sum(jnp.where(parent_front == parents[None, :], front_owner[None, :], 0), axis=1)
    rows_here = lax.dynamic_slice_in_dim(contrib_rows, place * share, share, 1) - place * height
    rows_here = jnp.where((target == column)[:, None], rows_here, -1).reshape(-1)
    selector = (
        lax.broadcasted_iota(jnp.int32, (height, rows_here.shape[0]), 0) == rows_here[None, :]
    ).astype(jnp.float32)
    positioned_rows = jnp.dot(
        selector,
        front_portions.reshape(-1, front_portions.shape[-1]),
        precision=EXACT,
        preferred_element_type=jnp.float32,
    )
    taken = jnp.max(selector, axis=1) > 0
    assembled = jnp.where(taken[:, None], positioned_rows, upper_rhs[0])
    upper_applied = wy_apply(assembled, upper_vectors[0], upper_factors[0, 0])
    upper_top, upper_back = run_tree(
        upper_applied[:width], summit_vectors[0, 0], summit_leads, blocks, place
    )
    upper_top = upper_top - product("ij,jn->in", summit_vectors[0, 0], upper_back)
    upper_result = lax.dynamic_update_slice(upper_applied, upper_top, (0, 0))[None]
    keep = (jnp.arange(width) < NPIV)[:, None] | (place != 0)
    lower = []
    for f in range(local_fronts):
        top, back = trees[f]
        top = top - product("ij,jn->in", merge_vectors[f, 0], back)
        lower.append(lax.dynamic_update_slice(applied[f], jnp.where(keep, top, 0.0), (0, 0)))
    return (jnp.stack(lower), upper_result)


def solution(mesh):
    placed = (
        P("fronts", "rows", None),
        P("fronts", "rows", None),
        P("fronts", "rows", None, None),
        P("fronts", "rows", None, None),
        P("fronts", "rows", None, None),
        P(),
        P(),
        P(),
        P(),
        P("fronts", "rows", None),
        P("fronts", "rows", None),
        P("fronts", "rows", None, None),
        P("fronts", "rows", None, None),
        P("fronts", "rows", None, None),
    )
    return jax.shard_map(
        per_device,
        mesh=mesh,
        in_specs=placed,
        out_specs=(P("fronts", "rows", None), P("fronts", "rows", None)),
        check_vma=False,
    )
```

```python
import functools

import jax
import jax.numpy as jnp
from jax import lax
from jax.experimental import pallas as pl
from jax.experimental.pallas import tpu as pltpu
from jax.sharding import PartitionSpec as P

NPIV = 128
CHUNK = 256
F32 = jnp.float32
BF16 = jnp.bfloat16


def split(x):
    high = x.astype(BF16)
    return high, (x - high.astype(F32)).astype(BF16)


def dot3(a, b, side):
    (ah, al), (bh, bl) = a, b
    dims = (((side,), (0,)), ((), ()))
    one = functools.partial(lax.dot_general, dimension_numbers=dims, preferred_element_type=F32)
    return one(ah, bh) + (one(ah, bl) + one(al, bh))


class Front:
    def __init__(self, blocks, x, vec, fac, nvec, nfac_any, s):
        self.blocks, self.levels = blocks, blocks.bit_length() - 1
        self.x, self.vec, self.fac, self.nvec, self.nfac_any = x, vec, fac, nvec, nfac_any
        (self.top, self.body, self.usend, self.urecv, self.wsend, self.wrecv, self.fin, self.lead,
         self.us, self.ur, self.ws, self.wr, self.gs, self.gr, self.fs) = s
        self.halves = x.shape[2] // CHUNK
        self.chunks = x.shape[0] * self.halves
        self.width = fac.shape[-1]
        self.place = lax.axis_index("rows")

    def role(self, level):
        step = 1 << level
        return self.place % (2 * step) == 0, self.place % (2 * step) == step, step

    def factor_copy(self, level, f, peer):
        return pltpu.make_async_remote_copy(
            self.nfac_any.at[f, 0], self.lead.at[level, f], self.gs.at[f], self.gr.at[level, f],
            device_id={"rows": peer}, device_id_type=pl.DeviceIdType.MESH)

    def send_factors(self):
        for level in range(self.levels):
            _, follow, step = self.role(level)

            @pl.when(follow)
            def _():
                for f in range(self.x.shape[0]):
                    self.factor_copy(level, f, self.place - step).start()

    def wait_factors(self):
        for level in range(self.levels):
            lead, _, step = self.role(level)

            @pl.when(lead)
            def _():
                for f in range(self.x.shape[0]):
                    self.factor_copy(level, f, self.place).wait_recv()

    def up_copy(self, level, c, peer):
        return pltpu.make_async_remote_copy(
            self.usend.at[c], self.urecv.at[level, c], self.us.at[c], self.ur.at[level, c],
            device_id={"rows": peer}, device_id_type=pl.DeviceIdType.MESH)

    def back_copy(self, level, c, peer):
        return pltpu.make_async_remote_copy(
            self.wsend.at[level, c], self.wrecv.at[c], self.ws.at[level, c], self.wr.at[c],
            device_id={"rows": peer}, device_id_type=pl.DeviceIdType.MESH)

    def send_up(self, level, c):
        _, follow, step = self.role(level)

        @pl.when(follow)
        def _():
            f = c // self.halves
            self.usend[c] = dot3(split(self.nvec[f, 0]), split(self.top[c]), 0)
            self.up_copy(level, c, self.place - step).start()

    def block(self, c, live):
        f, h = c // self.halves, c % self.halves
        columns = pl.ds(pl.multiple_of(h * CHUNK, CHUNK), CHUNK)
        x = self.x[f, :, columns]
        y = split(self.vec[f])
        project = dot3(y, split(x), 0)
        scaled = dot3(split(self.fac[f, 0]), split(project), 0)
        if live is not None:
            scaled = jnp.where(self.place < live(f), scaled, 0.0)
        z = split(scaled)
        w = self.width
        self.top[c] = x[:w] - dot3((y[0][:w], y[1][:w]), z, 1)
        self.body[c] = x[w:] - dot3((y[0][w:], y[1][w:]), z, 1)
        self.send_up(0, c)

    def climb(self, c, live):
        f = c // self.halves
        for level in range(self.levels):
            lead, _, step = self.role(level)
            if level:
                self.send_up(level, c)

            @pl.when(lead)
            def _():
                peer = self.place + step
                self.up_copy(level, c, peer).wait_recv()
                top = self.top[c]
                weight = dot3(split(self.lead[level, f]), split(top + self.urecv[level, c]), 0)
                if live is not None:
                    weight = jnp.where(peer < live(f), weight, 0.0)
                self.wsend[level, c] = weight
                self.back_copy(level, c, peer).start()
                self.top[c] = top - weight

    def finish(self, c, cut):
        f = c // self.halves

        @pl.when(self.place == 0)
        def _():
            top = self.top[c]
            if cut:
                rows = lax.broadcasted_iota(jnp.int32, top.shape, 0)
                top = jnp.where(rows < NPIV, top, 0.0)
            self.fin[c] = top

        @pl.when(self.place != 0)
        def _():
            self.back_copy(0, c, self.place).wait_recv()
            weight = split(self.wrecv[c])
            self.fin[c] = self.top[c] - dot3(split(self.nvec[f, 0]), weight, 1)

    def result_copies(self, out, c):
        f, h = c // self.halves, c % self.halves
        columns = pl.ds(pl.multiple_of(h * CHUNK, CHUNK), CHUNK)
        w, rows = self.width, self.x.shape[1]
        return (
            pltpu.make_async_copy(self.body.at[c], out.at[f, pl.ds(w, rows - w), columns], self.fs.at[0, c]),
            pltpu.make_async_copy(self.fin.at[c], out.at[f, pl.ds(0, w), columns], self.fs.at[1, c]),
        )

    def drain(self, out):
        for level in range(self.levels):
            lead, follow, _ = self.role(level)

            @pl.when(lead)
            def _():
                @pl.loop(0, self.chunks)
                def _(c):
                    self.back_copy(level, c, self.place).wait_send()

            @pl.when(follow)
            def _():
                for f in range(self.x.shape[0]):
                    self.factor_copy(level, f, self.place).wait_send()

                @pl.loop(0, self.chunks)
                def _(c):
                    self.up_copy(level, c, self.place).wait_send()

        @pl.loop(0, self.chunks)
        def _(c):
            for copy in self.result_copies(out, c):
                copy.wait()


def front_scratch(fronts, rows, cols, width, levels):
    chunks = fronts * (cols // CHUNK)
    piece = (width, CHUNK)
    dma = pltpu.SemaphoreType.DMA
    return [
        pltpu.VMEM((chunks,) + piece, F32),
        pltpu.VMEM((chunks, rows - width, CHUNK), F32),
        pltpu.VMEM((chunks,) + piece, F32),
        pltpu.VMEM((levels, chunks) + piece, F32),
        pltpu.VMEM((levels, chunks) + piece, F32),
        pltpu.VMEM((chunks,) + piece, F32),
        pltpu.VMEM((chunks,) + piece, F32),
        pltpu.VMEM((levels, fronts, width, width), F32),
        dma((chunks,)), dma((levels, chunks)), dma((levels, chunks)), dma((chunks,)),
        dma((fronts,)), dma((levels, fronts)), dma((2, chunks)),
    ]


def kernel(blocks, columns, rows_ref, live_ref, lx, lv, lf, mv, mf, ux, uv, uf, sv, sf, out_low, out_up, *s):
    place, column = lax.axis_index("rows"), lax.axis_index("fronts")
    vlx, vlv, vlf, vmv, vux, vuv, vuf, vsv, portions, load_sem, part_s, part_r, over_s, over_r = s[:14]
    low = Front(blocks, vlx, vlv, vlf, vmv, mf, s[14:29])
    up = Front(blocks, vux, vuv, vuf, vsv, sf, s[29:44])
    fronts = lx.shape[0]
    share = portions.shape[3]

    pairs = []
    for f in range(fronts):
        pairs += [(lx.at[f], vlx.at[f]), (lv.at[f], vlv.at[f]), (lf.at[f], vlf.at[f]), (mv.at[f], vmv.at[f])]
    first = len(pairs)
    pairs += [(ux, vux), (uv, vuv), (uf, vuf), (sv, vsv)]
    loads = [pltpu.make_async_copy(a, b, load_sem.at[i]) for i, (a, b) in enumerate(pairs)]
    for copy in loads:
        copy.start()

    barrier = pltpu.get_barrier_semaphore()
    for shift in range(1, blocks):
        pl.semaphore_signal(barrier, inc=1, device_id={"rows": (place + shift) % blocks},
                            device_id_type=pl.DeviceIdType.MESH)
    for shift in range(1, columns):
        pl.semaphore_signal(barrier, inc=1, device_id={"fronts": (column + shift) % columns},
                            device_id_type=pl.DeviceIdType.MESH)
    pl.semaphore_wait(barrier, blocks + columns - 2)
    low.send_factors()
    up.send_factors()

    def live(f):
        return live_ref[column * fronts + f]

    for copy in loads[:first]:
        copy.wait()

    @pl.loop(0, low.chunks)
    def _(c):
        low.block(c, live)
        low.result_copies(out_low, c)[0].start()

    low.wait_factors()

    def part(c, r, peer):
        f, h = c // low.halves, c % low.halves
        return pltpu.make_async_remote_copy(
            low.top.at[c, pl.ds(NPIV + r * share, share)], portions.at[column, f, h],
            part_s.at[r, c], part_r.at[c], device_id={"rows": peer}, device_id_type=pl.DeviceIdType.MESH)

    def over(c, shift, peer, slot):
        f, h = c // low.halves, c % low.halves
        return pltpu.make_async_remote_copy(
            portions.at[slot, f, h], portions.at[slot, f, h], over_s.at[shift, c], over_r.at[shift, c],
            device_id={"fronts": peer}, device_id_type=pl.DeviceIdType.MESH)

    @pl.loop(0, low.chunks)
    def _(c):
        low.climb(c, live)

        @pl.when(place == 0)
        def _():
            for r in range(1, blocks):
                part(c, r, r).start()
            portions[column, c // low.halves, c % low.halves] = low.top[c, pl.ds(NPIV, share)]

    for copy in loads[first:]:
        copy.wait()

    @pl.loop(0, low.chunks)
    def _(c):
        @pl.when(place != 0)
        def _():
            part(c, 0, place).wait_recv()

        for shift in range(1, columns):
            over(c, shift, (column + shift) % columns, column).start()

    @pl.loop(0, low.chunks)
    def _(c):
        low.finish(c, True)
        low.result_copies(out_low, c)[1].start()

    up.wait_factors()

    @pl.loop(0, low.chunks)
    def _(c):
        for shift in range(1, columns):
            over(c, shift, column, (column - shift + columns) % columns).wait_recv()

    height = vux.shape[1]
    here = rows_ref[...]
    hit = lax.broadcasted_iota(jnp.int32, (height, here.shape[1]), 0) == here
    chosen = jnp.where(hit, 1.0, 0.0)
    taken = jnp.sum(chosen, axis=1, keepdims=True) > 0.0
    chosen = chosen.astype(BF16)
    for h in range(low.halves):
        arrived = split(portions[:, :, h].reshape(here.shape[1], CHUNK))
        moved = jnp.dot(chosen, arrived[0], preferred_element_type=F32) + jnp.dot(
            chosen, arrived[1], preferred_element_type=F32)
        span = slice(h * CHUNK, (h + 1) * CHUNK)
        vux[0, :, span] = jnp.where(taken, moved, vux[0, :, span])

    @pl.loop(0, up.chunks)
    def _(c):
        up.block(c, None)
        up.result_copies(out_up, c)[0].start()

    @pl.loop(0, up.chunks)
    def _(c):
        up.climb(c, None)

    @pl.loop(0, up.chunks)
    def _(c):
        up.finish(c, False)
        up.result_copies(out_up, c)[1].start()

    @pl.when(place == 0)
    def _():
        @pl.loop(0, low.chunks)
        def _(c):
            for r in range(1, blocks):
                part(c, r, r).wait_send()

    @pl.loop(0, low.chunks)
    def _(c):
        for shift in range(1, columns):
            over(c, shift, column, column).wait_send()

    low.drain(out_low)
    up.drain(out_up)


def per_device(
    lower_rhs,
    lower_vectors,
    lower_factors,
    merge_vectors,
    merge_factors,
    live_blocks,
    parent_front,
    front_owner,
    contrib_rows,
    upper_rhs,
    upper_vectors,
    upper_factors,
    summit_vectors,
    summit_factors,
):
    place = lax.axis_index("rows")
    column = lax.axis_index("fronts")
    blocks = lax.axis_size("rows")
    columns = lax.axis_size("fronts")
    fronts, height, cols = lower_rhs.shape
    width = lower_factors.shape[-1]
    share = (width - NPIV) // blocks
    levels = blocks.bit_length() - 1
    parents = jnp.arange(front_owner.shape[0], dtype=jnp.int32)
    target = jnp.sum(jnp.where(parent_front == parents[None, :], front_owner[None, :], 0), axis=1)
    rows_here = lax.dynamic_slice_in_dim(contrib_rows, place * share, share, 1) - place * height
    rows_here = jnp.where((target == column)[:, None], rows_here, -1).reshape(1, -1)
    dma = pltpu.SemaphoreType.DMA
    chunks = fronts * (cols // CHUNK)
    held = [lower_rhs, lower_vectors, lower_factors, merge_vectors, upper_rhs, upper_vectors, upper_factors, summit_vectors]
    scratch = [pltpu.VMEM(a.shape, F32) for a in held]
    scratch += [
        pltpu.VMEM((columns, fronts, cols // CHUNK, share, CHUNK), F32),
        dma((4 * fronts + 4,)),
        dma((blocks, chunks)), dma((chunks,)), dma((columns, chunks)), dma((columns, chunks)),
    ]
    scratch += front_scratch(fronts, height, cols, width, levels)
    scratch += front_scratch(upper_rhs.shape[0], height, cols, width, levels)
    anywhere = pl.BlockSpec(memory_space=pl.ANY)
    return pl.pallas_call(
        functools.partial(kernel, blocks, columns),
        out_shape=(
            jax.ShapeDtypeStruct(lower_rhs.shape, F32),
            jax.ShapeDtypeStruct(upper_rhs.shape, F32),
        ),
        in_specs=[pl.BlockSpec(memory_space=pltpu.VMEM), pl.BlockSpec(memory_space=pltpu.SMEM)] + [anywhere] * 10,
        out_specs=(anywhere, anywhere),
        scratch_shapes=scratch,
        compiler_params=pltpu.CompilerParams(
            collective_id=0, has_side_effects=True, vmem_limit_bytes=56 * 1024 * 1024),
        name="two_level",
    )(rows_here, live_blocks, lower_rhs, lower_vectors, lower_factors, merge_vectors, merge_factors,
      upper_rhs, upper_vectors, upper_factors, summit_vectors, summit_factors)


def solution(mesh):
    placed = (
        P("fronts", "rows", None),
        P("fronts", "rows", None),
        P("fronts", "rows", None, None),
        P("fronts", "rows", None, None),
        P("fronts", "rows", None, None),
        P(),
        P(),
        P(),
        P(),
        P("fronts", "rows", None),
        P("fronts", "rows", None),
        P("fronts", "rows", None, None),
        P("fronts", "rows", None, None),
        P("fronts", "rows", None, None),
    )
    return jax.shard_map(
        per_device,
        mesh=mesh,
        in_specs=placed,
        out_specs=(P("fronts", "rows", None), P("fronts", "rows", None)),
        check_vma=False,
    )
```

```python
import functools

import jax
import jax.numpy as jnp
from jax import lax
from jax.experimental import pallas as pl
from jax.experimental.pallas import tpu as pltpu
from jax.sharding import PartitionSpec as P

NPIV = 128
LOW_CHUNK = 256
UP_CHUNK = 128
F32 = jnp.float32
BF16 = jnp.bfloat16


def split(x):
    high = x.astype(BF16)
    return high, (x - high.astype(F32)).astype(BF16)


def dot3(a, b, side):
    (ah, al), (bh, bl) = a, b
    dims = (((side,), (0,)), ((), ()))
    one = functools.partial(lax.dot_general, dimension_numbers=dims, preferred_element_type=F32)
    return one(ah, bh) + (one(ah, bl) + one(al, bh))


class Front:
    def __init__(self, blocks, x, vec, fac, nvec, nfac, nfac_any, chunk, s):
        self.blocks, self.levels, self.chunk = blocks, blocks.bit_length() - 1, chunk
        self.x, self.vec, self.fac, self.nvec, self.nfac, self.nfac_any = x, vec, fac, nvec, nfac, nfac_any
        (self.top, self.body, self.usend, self.urecv, self.wsend, self.wrecv, self.fin, self.hold,
         self.lead_in, self.rest_in, self.first,
         self.us, self.ur, self.ws, self.wr, self.ts, self.hs, self.li, self.ri,
         self.gs, self.gr, self.fs) = s
        self.halves = x.shape[2] // chunk
        self.chunks = x.shape[0] * self.halves
        self.width = fac.shape[-1]
        self.place = lax.axis_index("rows")
        self.odd = self.place % 2 == 1

    def remote(self, src, dst, send, recv, peer):
        return pltpu.make_async_remote_copy(
            src, dst, send, recv, device_id={"rows": peer}, device_id_type=pl.DeviceIdType.MESH)

    def factor_copy(self, f, peer):
        return self.remote(self.nfac_any.at[f, 0], self.first.at[f], self.gs.at[f], self.gr.at[f], peer)

    def send_factors(self):
        @pl.when(self.odd)
        def _():
            for f in range(self.x.shape[0]):
                self.factor_copy(f, self.place - 1).start()

    def wait_factors(self):
        @pl.when(~self.odd)
        def _():
            for f in range(self.x.shape[0]):
                self.factor_copy(f, self.place).wait_recv()

    def up_copy(self, c, peer):
        return self.remote(self.usend.at[c], self.urecv.at[c], self.us.at[c], self.ur.at[c], peer)

    def back_copy(self, c, peer):
        return self.remote(self.wsend.at[c], self.wrecv.at[c], self.ws.at[c], self.wr.at[c], peer)

    def top_copy(self, c, peer):
        return self.remote(self.top.at[c], self.lead_in.at[c], self.ts.at[c], self.li.at[c], peer)

    def lead_copy(self, c, peer):
        return self.remote(self.hold.at[c], self.lead_in.at[c], self.hs.at[c], self.li.at[c], peer)

    def rest_copy(self, c, peer):
        return self.remote(self.hold.at[c], self.rest_in.at[c], self.hs.at[c], self.ri.at[c], peer)

    def home_copy(self, c, rows):
        span = pl.ds(0, rows)
        return self.remote(self.hold.at[c, span], self.rest_in.at[c, span], self.hs.at[c], self.ri.at[c], 0)

    def block(self, c, live):
        f, h = c // self.halves, c % self.halves
        columns = pl.ds(pl.multiple_of(h * self.chunk, self.chunk), self.chunk)
        x = self.x[f, :, columns]
        y = split(self.vec[f])
        project = dot3(y, split(x), 0)
        scaled = dot3(split(self.fac[f, 0]), split(project), 0)
        if live is not None:
            scaled = jnp.where(self.place < live(f), scaled, 0.0)
        z = split(scaled)
        w = self.width
        self.top[c] = x[:w] - dot3((y[0][:w], y[1][:w]), z, 1)

        @pl.when(self.odd)
        def _():
            self.usend[c] = dot3(split(self.nvec[f, 0]), split(self.top[c]), 0)
            self.up_copy(c, self.place - 1).start()

        self.body[c] = x[w:] - dot3((y[0][w:], y[1][w:]), z, 1)

    def leaf(self, c, live):
        @pl.when(~self.odd)
        def _():
            f = c // self.halves
            peer = self.place + 1
            self.up_copy(c, peer).wait_recv()
            top = self.top[c]
            weight = dot3(split(self.first[f]), split(top + self.urecv[c]), 0)
            if live is not None:
                weight = jnp.where(peer < live(f), weight, 0.0)
            self.top[c] = top - weight

            @pl.when(self.place % 4 == 0)
            def _():
                self.top_copy(c, self.place + 2).start()

            self.wsend[c] = weight
            self.back_copy(c, peer).start()

    def node(self, level, c, live):
        step = 1 << level

        @pl.when(self.place % (2 * step) == step)
        def _():
            f = c // self.halves
            self.lead_copy(c, self.place).wait_recv()
            if level > 1:
                self.rest_copy(c, self.place).wait_recv()
            rest = self.top[c] if level == 1 else self.rest_in[c]
            lead = self.lead_in[c]
            vectors = split(self.nvec[f, 0])
            inner = lead + dot3(vectors, split(rest), 0)
            weight = dot3(split(self.nfac[f, 0]), split(inner), 0)
            if live is not None:
                weight = jnp.where(self.place < live(f), weight, 0.0)
            self.hold[c] = lead - weight
            if 2 * step < self.blocks:
                @pl.when(self.place % (4 * step) == step)
                def _():
                    self.lead_copy(c, self.place + step).start()

                @pl.when(self.place % (4 * step) == 3 * step)
                def _():
                    self.rest_copy(c, self.place - step).start()
            else:
                self.at_root(c)
            self.fin[c] = rest - dot3(vectors, split(weight), 1)

    def climb(self, live):
        @pl.loop(0, self.chunks + self.levels - 1)
        def _(i):
            @pl.when(i < self.chunks)
            def _():
                self.leaf(i, live)

            for level in range(1, self.levels):
                @pl.when((i >= level) & (i < self.chunks + level))
                def _():
                    self.node(level, i - level, live)

    def finish(self, c, home_rows):
        f = c // self.halves

        @pl.when(self.place == 0)
        def _():
            self.home_copy(c, home_rows).wait_recv()
            self.fin[c, pl.ds(0, home_rows)] = self.rest_in[c, pl.ds(0, home_rows)]
            if home_rows < self.width:
                self.fin[c, pl.ds(home_rows, self.width - home_rows)] = jnp.zeros(
                    (self.width - home_rows, self.chunk), F32)

        @pl.when(self.odd)
        def _():
            self.back_copy(c, self.place).wait_recv()
            self.fin[c] = self.top[c] - dot3(split(self.nvec[f, 0]), split(self.wrecv[c]), 1)

    def result_copies(self, out, c):
        f, h = c // self.halves, c % self.halves
        columns = pl.ds(pl.multiple_of(h * self.chunk, self.chunk), self.chunk)
        w, rows = self.width, self.x.shape[1]
        return (
            pltpu.make_async_copy(self.body.at[c], out.at[f, pl.ds(w, rows - w), columns], self.fs.at[0, c]),
            pltpu.make_async_copy(self.fin.at[c], out.at[f, pl.ds(0, w), columns], self.fs.at[1, c]),
        )

    def drain(self, out, home_rows):
        root = self.blocks // 2

        @pl.when(self.odd)
        def _():
            for f in range(self.x.shape[0]):
                self.factor_copy(f, self.place).wait_send()

        @pl.loop(0, self.chunks)
        def _(c):
            @pl.when(self.odd)
            def _():
                self.up_copy(c, self.place).wait_send()

            @pl.when(~self.odd)
            def _():
                self.back_copy(c, self.place).wait_send()

            @pl.when(self.place % 4 == 0)
            def _():
                self.top_copy(c, self.place).wait_send()

            @pl.when((~self.odd) & (self.place != 0) & (self.place != root))
            def _():
                self.lead_copy(c, self.place).wait_send()

            @pl.when(self.place == root)
            def _():
                self.home_copy(c, home_rows).wait_send()

            for copy in self.result_copies(out, c):
                copy.wait()


def front_scratch(fronts, rows, cols, width, chunk):
    chunks = fronts * (cols // chunk)
    dma = pltpu.SemaphoreType.DMA
    piece = pltpu.VMEM((chunks, width, chunk), F32)
    return (
        [piece, pltpu.VMEM((chunks, rows - width, chunk), F32)]
        + [piece] * 8
        + [pltpu.VMEM((fronts, width, width), F32)]
        + [dma((chunks,))] * 8
        + [dma((fronts,))] * 2
        + [dma((2, chunks))]
    )


def kernel(blocks, columns, rows_ref, live_ref, lx, lv, lf, mv, mf, ux, uv, uf, sv, sf, out_low, out_up, *s):
    place, column = lax.axis_index("rows"), lax.axis_index("fronts")
    vlx, vlv, vlf, vmv, vmf, vux, vuv, vuf, vsv, vsf, portions, load_sem, part_s, part_r, over_s, over_r = s[:16]
    low = Front(blocks, vlx, vlv, vlf, vmv, vmf, mf, LOW_CHUNK, s[16:38])
    up = Front(blocks, vux, vuv, vuf, vsv, vsf, sf, UP_CHUNK, s[38:60])
    fronts = lx.shape[0]
    share = portions.shape[3]
    root = blocks // 2

    pairs = []
    for f in range(fronts):
        pairs += [(lx.at[f], vlx.at[f]), (lv.at[f], vlv.at[f]), (lf.at[f], vlf.at[f]), (mv.at[f], vmv.at[f])]
    first = len(pairs)
    pairs += [(mf, vmf), (ux, vux), (uv, vuv), (uf, vuf), (sv, vsv), (sf, vsf)]
    loads = [pltpu.make_async_copy(a, b, load_sem.at[i]) for i, (a, b) in enumerate(pairs)]
    for copy in loads:
        copy.start()

    barrier = pltpu.get_barrier_semaphore()
    for shift in range(1, blocks):
        pl.semaphore_signal(barrier, inc=1, device_id={"rows": (place + shift) % blocks},
                            device_id_type=pl.DeviceIdType.MESH)
    for shift in range(1, columns):
        pl.semaphore_signal(barrier, inc=1, device_id={"fronts": (column + shift) % columns},
                            device_id_type=pl.DeviceIdType.MESH)
    pl.semaphore_wait(barrier, blocks + columns - 2)
    low.send_factors()

    def live(f):
        return live_ref[column * fronts + f]

    for f in range(fronts):
        for copy in loads[4 * f:4 * f + 4]:
            copy.wait()

        @pl.loop(f * low.halves, (f + 1) * low.halves)
        def _(c):
            low.block(c, live)
            low.result_copies(out_low, c)[0].start()

    up.send_factors()
    for copy in loads[first:]:
        copy.wait()
    low.wait_factors()

    def part(c, r, peer):
        f, h = c // low.halves, c % low.halves
        return low.remote(
            low.hold.at[c, pl.ds(NPIV + r * share, share)], portions.at[column, f, h],
            part_s.at[r, c], part_r.at[c], peer)

    def over(c, shift, peer, slot):
        f, h = c // low.halves, c % low.halves
        return pltpu.make_async_remote_copy(
            portions.at[slot, f, h], portions.at[slot, f, h], over_s.at[shift, c], over_r.at[shift, c],
            device_id={"fronts": peer}, device_id_type=pl.DeviceIdType.MESH)

    def spread(c):
        for r in range(blocks):
            if r != root:
                part(c, r, r).start()
        portions[column, c // low.halves, c % low.halves] = low.hold[c, pl.ds(NPIV + root * share, share)]

    low.at_root = spread
    up.at_root = lambda c: up.home_copy(c, up.width).start()

    low.climb(live)

    @pl.loop(0, low.chunks)
    def _(c):
        @pl.when(place != root)
        def _():
            part(c, 0, place).wait_recv()

        for shift in range(1, columns):
            over(c, shift, (column + shift) % columns, column).start()

    @pl.when(place == root)
    def _():
        @pl.loop(0, low.chunks)
        def _(c):
            low.home_copy(c, NPIV).start()

    up.wait_factors()

    @pl.loop(0, low.chunks)
    def _(c):
        for shift in range(1, columns):
            over(c, shift, column, (column - shift + columns) % columns).wait_recv()

    height = vux.shape[1]
    here = rows_ref[...]
    hit = lax.broadcasted_iota(jnp.int32, (height, here.shape[1]), 0) == here
    chosen = jnp.where(hit, 1.0, 0.0)
    taken = jnp.sum(chosen, axis=1, keepdims=True) > 0.0
    chosen = chosen.astype(BF16)
    for h in range(low.halves):
        arrived = split(portions[:, :, h].reshape(here.shape[1], LOW_CHUNK))
        moved = jnp.dot(chosen, arrived[0], preferred_element_type=F32) + jnp.dot(
            chosen, arrived[1], preferred_element_type=F32)
        span = slice(h * LOW_CHUNK, (h + 1) * LOW_CHUNK)
        vux[0, :, span] = jnp.where(taken, moved, vux[0, :, span])

    @pl.loop(0, up.chunks)
    def _(c):
        up.block(c, None)
        up.result_copies(out_up, c)[0].start()

    up.climb(None)

    @pl.loop(0, low.chunks)
    def _(c):
        low.finish(c, NPIV)
        low.result_copies(out_low, c)[1].start()

    @pl.loop(0, up.chunks)
    def _(c):
        up.finish(c, up.width)
        up.result_copies(out_up, c)[1].start()

    @pl.when(place == root)
    def _():
        @pl.loop(0, low.chunks)
        def _(c):
            for r in range(blocks):
                if r != root:
                    part(c, r, r).wait_send()

    @pl.loop(0, low.chunks)
    def _(c):
        for shift in range(1, columns):
            over(c, shift, column, column).wait_send()

    low.drain(out_low, NPIV)
    up.drain(out_up, up.width)


def per_device(
    lower_rhs,
    lower_vectors,
    lower_factors,
    merge_vectors,
    merge_factors,
    live_blocks,
    parent_front,
    front_owner,
    contrib_rows,
    upper_rhs,
    upper_vectors,
    upper_factors,
    summit_vectors,
    summit_factors,
):
    place = lax.axis_index("rows")
    column = lax.axis_index("fronts")
    blocks = lax.axis_size("rows")
    columns = lax.axis_size("fronts")
    fronts, height, cols = lower_rhs.shape
    width = lower_factors.shape[-1]
    share = (width - NPIV) // blocks
    parents = jnp.arange(front_owner.shape[0], dtype=jnp.int32)
    target = jnp.sum(jnp.where(parent_front == parents[None, :], front_owner[None, :], 0), axis=1)
    rows_here = lax.dynamic_slice_in_dim(contrib_rows, place * share, share, 1) - place * height
    rows_here = jnp.where((target == column)[:, None], rows_here, -1).reshape(1, -1)
    dma = pltpu.SemaphoreType.DMA
    chunks = fronts * (cols // LOW_CHUNK)
    held = [lower_rhs, lower_vectors, lower_factors, merge_vectors, merge_factors]
    held += [upper_rhs, upper_vectors, upper_factors, summit_vectors, summit_factors]
    scratch = [pltpu.VMEM(a.shape, F32) for a in held]
    scratch += [
        pltpu.VMEM((columns, fronts, cols // LOW_CHUNK, share, LOW_CHUNK), F32),
        dma((4 * fronts + 6,)),
        dma((blocks, chunks)), dma((chunks,)), dma((columns, chunks)), dma((columns, chunks)),
    ]
    scratch += front_scratch(fronts, height, cols, width, LOW_CHUNK)
    scratch += front_scratch(upper_rhs.shape[0], height, cols, width, UP_CHUNK)
    anywhere = pl.BlockSpec(memory_space=pl.ANY)
    return pl.pallas_call(
        functools.partial(kernel, blocks, columns),
        out_shape=(
            jax.ShapeDtypeStruct(lower_rhs.shape, F32),
            jax.ShapeDtypeStruct(upper_rhs.shape, F32),
        ),
        in_specs=[pl.BlockSpec(memory_space=pltpu.VMEM), pl.BlockSpec(memory_space=pltpu.SMEM)] + [anywhere] * 10,
        out_specs=(anywhere, anywhere),
        scratch_shapes=scratch,
        compiler_params=pltpu.CompilerParams(
            collective_id=0, has_side_effects=True, vmem_limit_bytes=56 * 1024 * 1024),
        name="two_level",
    )(rows_here, live_blocks, lower_rhs, lower_vectors, lower_factors, merge_vectors, merge_factors,
      upper_rhs, upper_vectors, upper_factors, summit_vectors, summit_factors)


def solution(mesh):
    placed = (
        P("fronts", "rows", None),
        P("fronts", "rows", None),
        P("fronts", "rows", None, None),
        P("fronts", "rows", None, None),
        P("fronts", "rows", None, None),
        P(),
        P(),
        P(),
        P(),
        P("fronts", "rows", None),
        P("fronts", "rows", None),
        P("fronts", "rows", None, None),
        P("fronts", "rows", None, None),
        P("fronts", "rows", None, None),
    )
    return jax.shard_map(
        per_device,
        mesh=mesh,
        in_specs=placed,
        out_specs=(P("fronts", "rows", None), P("fronts", "rows", None)),
        check_vma=False,
    )
```

```python
import functools

import jax
import jax.numpy as jnp
from jax import lax
from jax.experimental import pallas as pl
from jax.experimental.pallas import tpu as pltpu
from jax.sharding import PartitionSpec as P

NPIV = 128
LOW_CHUNK = 256
UP_CHUNK = 128
F32 = jnp.float32
BF16 = jnp.bfloat16


def split(x):
    high = x.astype(BF16)
    return high, (x - high.astype(F32)).astype(BF16)


def dot3(a, b, side):
    (ah, al), (bh, bl) = a, b
    dims = (((side,), (0,)), ((), ()))
    one = functools.partial(lax.dot_general, dimension_numbers=dims, preferred_element_type=F32)
    return one(ah, bh) + (one(ah, bl) + one(al, bh))


class Front:
    def __init__(self, blocks, x, vec, fac, nvec, nfac, nfac_any, chunk, s):
        self.blocks, self.levels, self.chunk = blocks, blocks.bit_length() - 1, chunk
        self.x, self.vec, self.fac, self.nvec, self.nfac, self.nfac_any = x, vec, fac, nvec, nfac, nfac_any
        (self.top, self.body, self.usend, self.urecv, self.wsend, self.wrecv, self.fin, self.hold,
         self.lead_in, self.rest_in, self.scaled, self.first,
         self.us, self.ur, self.ws, self.wr, self.ts, self.hs, self.li, self.ri,
         self.gs, self.gr, self.fs) = s
        self.halves = x.shape[2] // chunk
        self.fronts = x.shape[0]
        self.chunks = self.fronts * self.halves
        self.width = fac.shape[-1]
        self.place = lax.axis_index("rows")
        self.odd = self.place % 2 == 1

    def remote(self, src, dst, send, recv, peer):
        return pltpu.make_async_remote_copy(
            src, dst, send, recv, device_id={"rows": peer}, device_id_type=pl.DeviceIdType.MESH)

    def factor_copy(self, f, peer):
        return self.remote(self.nfac_any.at[f, 0], self.first.at[f], self.gs.at[f], self.gr.at[f], peer)

    def send_factors(self):
        @pl.when(self.odd)
        def _():
            for f in range(self.x.shape[0]):
                self.factor_copy(f, self.place - 1).start()

    def wait_factors(self):
        @pl.when(~self.odd)
        def _():
            for f in range(self.x.shape[0]):
                self.factor_copy(f, self.place).wait_recv()

    def up_copy(self, c, peer):
        return self.remote(self.usend.at[c], self.urecv.at[c], self.us.at[c], self.ur.at[c], peer)

    def back_copy(self, c, peer):
        return self.remote(self.wsend.at[c], self.wrecv.at[c], self.ws.at[c], self.wr.at[c], peer)

    def top_copy(self, c, peer):
        return self.remote(self.top.at[c], self.lead_in.at[c], self.ts.at[c], self.li.at[c], peer)

    def lead_copy(self, c, peer):
        return self.remote(self.hold.at[c], self.lead_in.at[c], self.hs.at[c], self.li.at[c], peer)

    def rest_copy(self, c, peer):
        return self.remote(self.hold.at[c], self.rest_in.at[c], self.hs.at[c], self.ri.at[c], peer)

    def home_copy(self, c, rows):
        span = pl.ds(0, rows)
        return self.remote(self.hold.at[c, span], self.rest_in.at[c, span], self.hs.at[c], self.ri.at[c], 0)

    def tops(self, c, live, taken=None):
        f, h = c % self.fronts, c // self.fronts
        columns = pl.ds(pl.multiple_of(h * self.chunk, self.chunk), self.chunk)
        x = self.x[f, :, columns]
        if taken is not None:
            x = jnp.where(taken, 0.0, x)
            self.x[f, :, columns] = x
        y = split(self.vec[f])
        project = dot3(y, split(x), 0)
        scaled = dot3(split(self.fac[f, 0]), split(project), 0)
        if live is not None:
            scaled = jnp.where(self.place < live(f), scaled, 0.0)
        self.scaled[c] = scaled
        w = self.width
        self.top[c] = x[:w] - dot3((y[0][:w], y[1][:w]), split(scaled), 1)

    def send_up(self, c):
        f = c % self.fronts

        @pl.when(self.odd)
        def _():
            self.usend[c] = dot3(split(self.nvec[f, 0]), split(self.top[c]), 0)
            self.up_copy(c, self.place - 1).start()

    def bodies(self, c):
        f, h = c % self.fronts, c // self.fronts
        columns = pl.ds(pl.multiple_of(h * self.chunk, self.chunk), self.chunk)
        w = self.width
        lower = pl.ds(w, self.x.shape[1] - w)
        self.body[c] = self.x[f, lower, columns] - dot3(split(self.vec[f, lower]), split(self.scaled[c]), 1)

    def leaf(self, c, live):
        @pl.when(~self.odd)
        def _():
            f = c % self.fronts
            peer = self.place + 1
            self.up_copy(c, peer).wait_recv()
            top = self.top[c]
            weight = dot3(split(self.first[f]), split(top + self.urecv[c]), 0)
            if live is not None:
                weight = jnp.where(peer < live(f), weight, 0.0)
            self.top[c] = top - weight

            @pl.when(self.place % 4 == 0)
            def _():
                self.top_copy(c, self.place + 2).start()

            self.wsend[c] = weight
            self.back_copy(c, peer).start()

    def node(self, level, c, live):
        step = 1 << level

        @pl.when(self.place % (2 * step) == step)
        def _():
            f = c % self.fronts
            self.lead_copy(c, self.place).wait_recv()
            if level > 1:
                self.rest_copy(c, self.place).wait_recv()
            rest = self.top[c] if level == 1 else self.rest_in[c]
            lead = self.lead_in[c]
            vectors = split(self.nvec[f, 0])
            inner = lead + dot3(vectors, split(rest), 0)
            weight = dot3(split(self.nfac[f, 0]), split(inner), 0)
            if live is not None:
                weight = jnp.where(self.place < live(f), weight, 0.0)
            self.hold[c] = lead - weight
            if 2 * step < self.blocks:
                @pl.when(self.place % (4 * step) == step)
                def _():
                    self.lead_copy(c, self.place + step).start()

                @pl.when(self.place % (4 * step) == 3 * step)
                def _():
                    self.rest_copy(c, self.place - step).start()
            else:
                self.at_root(c)
            self.fin[c] = rest - dot3(vectors, split(weight), 1)

    def climb(self, live):
        @pl.loop(0, self.chunks + self.levels - 1)
        def _(i):
            @pl.when(i < self.chunks)
            def _():
                self.leaf(i, live)

            for level in range(1, self.levels):
                @pl.when((i >= level) & (i < self.chunks + level))
                def _():
                    self.node(level, i - level, live)

    def finish(self, c, home_rows):
        f = c % self.fronts

        @pl.when(self.place == 0)
        def _():
            self.home_copy(c, home_rows).wait_recv()
            self.fin[c, pl.ds(0, home_rows)] = self.rest_in[c, pl.ds(0, home_rows)]
            if home_rows < self.width:
                self.fin[c, pl.ds(home_rows, self.width - home_rows)] = jnp.zeros(
                    (self.width - home_rows, self.chunk), F32)

        @pl.when(self.odd)
        def _():
            self.back_copy(c, self.place).wait_recv()
            self.fin[c] = self.top[c] - dot3(split(self.nvec[f, 0]), split(self.wrecv[c]), 1)

    def result_copies(self, out, c):
        f, h = c % self.fronts, c // self.fronts
        columns = pl.ds(pl.multiple_of(h * self.chunk, self.chunk), self.chunk)
        w, rows = self.width, self.x.shape[1]
        return (
            pltpu.make_async_copy(self.body.at[c], out.at[f, pl.ds(w, rows - w), columns], self.fs.at[0, c]),
            pltpu.make_async_copy(self.fin.at[c], out.at[f, pl.ds(0, w), columns], self.fs.at[1, c]),
        )

    def drain(self, out, home_rows):
        root = self.blocks // 2

        @pl.when(self.odd)
        def _():
            for f in range(self.x.shape[0]):
                self.factor_copy(f, self.place).wait_send()

        @pl.loop(0, self.chunks)
        def _(c):
            @pl.when(self.odd)
            def _():
                self.up_copy(c, self.place).wait_send()

            @pl.when(~self.odd)
            def _():
                self.back_copy(c, self.place).wait_send()

            @pl.when(self.place % 4 == 0)
            def _():
                self.top_copy(c, self.place).wait_send()

            @pl.when((~self.odd) & (self.place != 0) & (self.place != root))
            def _():
                self.lead_copy(c, self.place).wait_send()

            @pl.when(self.place == root)
            def _():
                self.home_copy(c, home_rows).wait_send()

            for copy in self.result_copies(out, c):
                copy.wait()


def front_scratch(fronts, rows, cols, width, chunk):
    chunks = fronts * (cols // chunk)
    dma = pltpu.SemaphoreType.DMA
    piece = pltpu.VMEM((chunks, width, chunk), F32)
    return (
        [piece, pltpu.VMEM((chunks, rows - width, chunk), F32)]
        + [piece] * 9
        + [pltpu.VMEM((fronts, width, width), F32)]
        + [dma((chunks,))] * 8
        + [dma((fronts,))] * 2
        + [dma((2, chunks))]
    )


def kernel(blocks, columns, rows_ref, live_ref, parent_ref, owner_ref, lx, lv, lf, mv, mf, ux, uv, uf, sv, sf, out_low, out_up, *s):
    place, column = lax.axis_index("rows"), lax.axis_index("fronts")
    vlx, vlv, vlf, vmv, vmf, vux, vuv, vuf, vsv, vsf, portions, tmat, load_sem, part_s, part_r, over_s, over_r = s[:17]
    low = Front(blocks, vlx, vlv, vlf, vmv, vmf, mf, LOW_CHUNK, s[17:40])
    up = Front(blocks, vux, vuv, vuf, vsv, vsf, sf, UP_CHUNK, s[40:63])
    fronts = lx.shape[0]
    share = portions.shape[3]
    root = blocks // 2

    pairs = []
    for f in range(fronts):
        pairs += [(lx.at[f], vlx.at[f]), (lv.at[f], vlv.at[f]), (lf.at[f], vlf.at[f]), (mv.at[f], vmv.at[f])]
    first = len(pairs)
    pairs += [(mf, vmf), (ux, vux), (uv, vuv), (uf, vuf), (sv, vsv), (sf, vsf)]
    loads = [pltpu.make_async_copy(a, b, load_sem.at[i]) for i, (a, b) in enumerate(pairs)]
    for copy in loads:
        copy.start()

    barrier = pltpu.get_barrier_semaphore()
    for shift in range(1, blocks):
        pl.semaphore_signal(barrier, inc=1, device_id={"rows": (place + shift) % blocks},
                            device_id_type=pl.DeviceIdType.MESH)
    for shift in range(1, columns):
        pl.semaphore_signal(barrier, inc=1, device_id={"fronts": (column + shift) % columns},
                            device_id_type=pl.DeviceIdType.MESH)
    pl.semaphore_wait(barrier, blocks + columns - 2)
    low.send_factors()

    def live(f):
        return live_ref[column * fronts + f]

    for f in range(fronts):
        for copy in loads[4 * f:4 * f + 4]:
            copy.wait()
        low.tops(f, live)
        low.send_up(f)

    @pl.loop(fronts, low.chunks)
    def _(c):
        low.tops(c, live)
        low.send_up(c)

    up.send_factors()

    @pl.loop(0, low.chunks)
    def _(c):
        low.bodies(c)
        low.result_copies(out_low, c)[0].start()

    for copy in loads[first:]:
        copy.wait()

    height, total = vux.shape[1], rows_ref.shape[0]
    lanes = rows_ref.shape[1]
    spots = total * share
    mine = jnp.broadcast_to(rows_ref[...].astype(F32)[:, None, :], (total, share, lanes)).reshape(spots, lanes)
    spot = lax.broadcasted_iota(jnp.int32, (spots, lanes), 0)
    lane = lax.broadcasted_iota(jnp.int32, (spots, lanes), 1)
    child = spot // share
    here_too = jnp.zeros((spots, lanes), F32)
    for c in range(total):
        owned = jnp.where(owner_ref[parent_ref[c, 0]] == column, 1.0, 0.0)
        here_too = jnp.where(child == c, owned, here_too)
    wanted = (lane == place * share + spot % share) & (here_too > 0.0)
    base = (place * height).astype(F32)
    offset = jnp.sum(jnp.where(wanted, mine - base + 1.0, 0.0), axis=1, keepdims=True) - 1.0
    here = jnp.broadcast_to(offset, (spots, spots)).T[0:1]
    hit = lax.broadcasted_iota(jnp.int32, (height, spots), 0).astype(F32) == here
    chosen = jnp.where(hit, 1.0, 0.0)
    taken = jnp.sum(chosen, axis=1, keepdims=True) > 0.0
    y = split(vuv[0])
    one = chosen.astype(BF16)
    down = (((0,), (0,)), ((), ()))
    gram = lax.dot_general(y[0], one, down, preferred_element_type=F32) + lax.dot_general(
        y[1], one, down, preferred_element_type=F32)
    inner = split(dot3(split(vuf[0, 0]), split(gram), 0))
    tmat[...] = chosen - dot3(y, inner, 1)

    @pl.loop(0, up.chunks)
    def _(c):
        up.tops(c, None, taken)
        up.bodies(c)

    low.wait_factors()

    def part(c, r, peer):
        f, h = c % fronts, c // fronts
        return low.remote(
            low.hold.at[c, pl.ds(NPIV + r * share, share)], portions.at[column, f, h],
            part_s.at[r, c], part_r.at[c], peer)

    def over(c, shift, peer, slot):
        f, h = c % fronts, c // fronts
        return pltpu.make_async_remote_copy(
            portions.at[slot, f, h], portions.at[slot, f, h], over_s.at[shift, c], over_r.at[shift, c],
            device_id={"fronts": peer}, device_id_type=pl.DeviceIdType.MESH)

    def spread(c):
        for r in range(blocks):
            if r != root:
                part(c, r, r).start()
        portions[column, c % fronts, c // fronts] = low.hold[c, pl.ds(NPIV + root * share, share)]

    low.at_root = spread
    up.at_root = lambda c: up.home_copy(c, up.width).start()

    low.climb(live)

    @pl.loop(0, low.chunks)
    def _(c):
        @pl.when(place != root)
        def _():
            part(c, 0, place).wait_recv()

        for shift in range(1, columns):
            over(c, shift, (column + shift) % columns, column).start()

    @pl.when(place == root)
    def _():
        @pl.loop(0, low.chunks)
        def _(c):
            low.home_copy(c, NPIV).start()

    inside = LOW_CHUNK // UP_CHUNK

    for h in range(low.halves):
        for f in range(fronts):
            for shift in range(1, columns):
                over(h * fronts + f, shift, column, (column - shift + columns) % columns).wait_recv()
        arrived = split(portions[:, :, h].reshape(spots, LOW_CHUNK))
        gained = dot3(split(tmat[pl.ds(0, up.width)]), arrived, 1)
        for k in range(inside):
            c = h * inside + k
            up.top[c] += gained[:, k * UP_CHUNK:(k + 1) * UP_CHUNK]
            up.send_up(c)

    @pl.loop(0, up.chunks)
    def _(c):
        h, k = c // inside, c % inside
        arrived = split(portions[:, :, h, :, pl.ds(pl.multiple_of(k * UP_CHUNK, UP_CHUNK), UP_CHUNK)].reshape(spots, UP_CHUNK))
        up.body[c] += dot3(split(tmat[pl.ds(up.width, height - up.width)]), arrived, 1)
        up.result_copies(out_up, c)[0].start()

    up.wait_factors()
    up.climb(None)

    @pl.loop(0, low.chunks)
    def _(c):
        low.finish(c, NPIV)
        low.result_copies(out_low, c)[1].start()

    @pl.loop(0, up.chunks)
    def _(c):
        up.finish(c, up.width)
        up.result_copies(out_up, c)[1].start()

    @pl.when(place == root)
    def _():
        @pl.loop(0, low.chunks)
        def _(c):
            for r in range(blocks):
                if r != root:
                    part(c, r, r).wait_send()

    @pl.loop(0, low.chunks)
    def _(c):
        for shift in range(1, columns):
            over(c, shift, column, column).wait_send()

    low.drain(out_low, NPIV)
    up.drain(out_up, up.width)


def per_device(
    lower_rhs,
    lower_vectors,
    lower_factors,
    merge_vectors,
    merge_factors,
    live_blocks,
    parent_front,
    front_owner,
    contrib_rows,
    upper_rhs,
    upper_vectors,
    upper_factors,
    summit_vectors,
    summit_factors,
):
    blocks = lax.axis_size("rows")
    columns = lax.axis_size("fronts")
    fronts, height, cols = lower_rhs.shape
    width = lower_factors.shape[-1]
    share = (width - NPIV) // blocks
    dma = pltpu.SemaphoreType.DMA
    chunks = fronts * (cols // LOW_CHUNK)
    held = [lower_rhs, lower_vectors, lower_factors, merge_vectors, merge_factors]
    held += [upper_rhs, upper_vectors, upper_factors, summit_vectors, summit_factors]
    scratch = [pltpu.VMEM(a.shape, F32) for a in held]
    scratch += [
        pltpu.VMEM((columns, fronts, cols // LOW_CHUNK, share, LOW_CHUNK), F32),
        pltpu.VMEM((height, contrib_rows.shape[0] * share), F32),
        dma((4 * fronts + 6,)),
        dma((blocks, chunks)), dma((chunks,)), dma((columns, chunks)), dma((columns, chunks)),
    ]
    scratch += front_scratch(fronts, height, cols, width, LOW_CHUNK)
    scratch += front_scratch(upper_rhs.shape[0], height, cols, width, UP_CHUNK)
    anywhere = pl.BlockSpec(memory_space=pl.ANY)
    return pl.pallas_call(
        functools.partial(kernel, blocks, columns),
        out_shape=(
            jax.ShapeDtypeStruct(lower_rhs.shape, F32),
            jax.ShapeDtypeStruct(upper_rhs.shape, F32),
        ),
        in_specs=[pl.BlockSpec(memory_space=pltpu.VMEM)] + [pl.BlockSpec(memory_space=pltpu.SMEM)] * 3 + [anywhere] * 10,
        out_specs=(anywhere, anywhere),
        scratch_shapes=scratch,
        compiler_params=pltpu.CompilerParams(
            collective_id=0, has_side_effects=True, vmem_limit_bytes=56 * 1024 * 1024),
        name="two_level",
    )(contrib_rows, live_blocks, parent_front, front_owner, lower_rhs, lower_vectors, lower_factors, merge_vectors, merge_factors,
      upper_rhs, upper_vectors, upper_factors, summit_vectors, summit_factors)


def solution(mesh):
    placed = (
        P("fronts", "rows", None),
        P("fronts", "rows", None),
        P("fronts", "rows", None, None),
        P("fronts", "rows", None, None),
        P("fronts", "rows", None, None),
        P(),
        P(),
        P(),
        P(),
        P("fronts", "rows", None),
        P("fronts", "rows", None),
        P("fronts", "rows", None, None),
        P("fronts", "rows", None, None),
        P("fronts", "rows", None, None),
    )
    return jax.shard_map(
        per_device,
        mesh=mesh,
        in_specs=placed,
        out_specs=(P("fronts", "rows", None), P("fronts", "rows", None)),
        check_vma=False,
    )
```

```python
import functools

import jax
import jax.numpy as jnp
from jax import lax
from jax.experimental import pallas as pl
from jax.experimental.pallas import tpu as pltpu
from jax.sharding import PartitionSpec as P

NPIV = 128
LOW_CHUNK = 256
UP_CHUNK = 128
F32 = jnp.float32
BF16 = jnp.bfloat16


def split(x):
    high = x.astype(BF16)
    return high, (x - high.astype(F32)).astype(BF16)


def pair(ref, f):
    return ref[0, f], ref[1, f]


def dot3(a, b):
    (ah, al), (bh, bl) = a, b
    one = functools.partial(jnp.dot, preferred_element_type=F32)
    return one(ah, bh) + (one(ah, bl) + one(al, bh))


class Front:
    def __init__(self, blocks, x, vec, fac, nvec, nfac, nfac_any, chunk, s):
        self.blocks, self.levels, self.chunk = blocks, blocks.bit_length() - 1, chunk
        self.x, self.vec, self.fac, self.nvec, self.nfac, self.nfac_any = x, vec, fac, nvec, nfac, nfac_any
        (self.top, self.body, self.usend, self.urecv, self.wsend, self.wrecv, self.fin, self.hold,
         self.lead_in, self.rest_in, self.scaled, self.first,
         self.yt, self.vt, self.gt, self.ft, self.first_t,
         self.us, self.ur, self.ws, self.wr, self.ts, self.hs, self.li, self.ri,
         self.gs, self.gr, self.fs) = s
        self.halves = x.shape[2] // chunk
        self.fronts = x.shape[0]
        self.chunks = self.fronts * self.halves
        self.width = fac.shape[-1]
        self.place = lax.axis_index("rows")
        self.odd = self.place % 2 == 1

    def remote(self, src, dst, send, recv, peer):
        return pltpu.make_async_remote_copy(
            src, dst, send, recv, device_id={"rows": peer}, device_id_type=pl.DeviceIdType.MESH)

    def factor_copy(self, f, peer):
        return self.remote(self.nfac_any.at[f, 0], self.first.at[f], self.gs.at[f], self.gr.at[f], peer)

    def send_factors(self):
        @pl.when(self.odd)
        def _():
            for f in range(self.x.shape[0]):
                self.factor_copy(f, self.place - 1).start()

    def wait_factors(self):
        @pl.when(~self.odd)
        def _():
            for f in range(self.x.shape[0]):
                self.factor_copy(f, self.place).wait_recv()
                self.keep(self.first_t, f, self.first[f])

    def keep(self, ref, f, value):
        ref[0, f], ref[1, f] = split(value.T)

    def turn(self, f):
        self.keep(self.yt, f, self.vec[f])
        self.keep(self.ft, f, self.fac[f, 0])
        self.keep(self.vt, f, self.nvec[f, 0])

    def turn_nodes(self):
        for f in range(self.x.shape[0]):
            self.keep(self.gt, f, self.nfac[f, 0])

    def up_copy(self, c, peer):
        return self.remote(self.usend.at[c], self.urecv.at[c], self.us.at[c], self.ur.at[c], peer)

    def back_copy(self, c, peer):
        return self.remote(self.wsend.at[c], self.wrecv.at[c], self.ws.at[c], self.wr.at[c], peer)

    def top_copy(self, c, peer):
        return self.remote(self.top.at[c], self.lead_in.at[c], self.ts.at[c], self.li.at[c], peer)

    def lead_copy(self, c, peer):
        return self.remote(self.hold.at[c], self.lead_in.at[c], self.hs.at[c], self.li.at[c], peer)

    def rest_copy(self, c, peer):
        return self.remote(self.hold.at[c], self.rest_in.at[c], self.hs.at[c], self.ri.at[c], peer)

    def home_copy(self, c, rows):
        span = pl.ds(0, rows)
        return self.remote(self.hold.at[c, span], self.rest_in.at[c, span], self.hs.at[c], self.ri.at[c], 0)

    def tops(self, c, live):
        f, h = c % self.fronts, c // self.fronts
        columns = pl.ds(pl.multiple_of(h * self.chunk, self.chunk), self.chunk)
        x = self.x[f, :, columns]
        project = dot3(pair(self.yt, f), split(x))
        scaled = dot3(pair(self.ft, f), split(project))
        if live is not None:
            scaled = jnp.where(self.place < live(f), scaled, 0.0)
        self.scaled[c] = scaled
        w = self.width
        self.top[c] = x[:w] - dot3(split(self.vec[f, pl.ds(0, w)]), split(scaled))

    def send_up(self, c):
        f = c % self.fronts

        @pl.when(self.odd)
        def _():
            self.usend[c] = dot3(pair(self.vt, f), split(self.top[c]))
            self.up_copy(c, self.place - 1).start()

    def bodies(self, c):
        f, h = c % self.fronts, c // self.fronts
        columns = pl.ds(pl.multiple_of(h * self.chunk, self.chunk), self.chunk)
        w = self.width
        lower = pl.ds(w, self.x.shape[1] - w)
        self.body[c] = self.x[f, lower, columns] - dot3(split(self.vec[f, lower]), split(self.scaled[c]))

    def leaf(self, c, live):
        @pl.when(~self.odd)
        def _():
            f = c % self.fronts
            peer = self.place + 1
            self.up_copy(c, peer).wait_recv()
            top = self.top[c]
            weight = dot3(pair(self.first_t, f), split(top + self.urecv[c]))
            if live is not None:
                weight = jnp.where(peer < live(f), weight, 0.0)
            self.top[c] = top - weight

            @pl.when(self.place % 4 == 0)
            def _():
                self.top_copy(c, self.place + 2).start()

            self.wsend[c] = weight
            self.back_copy(c, peer).start()

    def node(self, level, c, live):
        step = 1 << level

        @pl.when(self.place % (2 * step) == step)
        def _():
            f = c % self.fronts
            self.lead_copy(c, self.place).wait_recv()
            if level > 1:
                self.rest_copy(c, self.place).wait_recv()
            rest = self.top[c] if level == 1 else self.rest_in[c]
            lead = self.lead_in[c]
            inner = lead + dot3(pair(self.vt, f), split(rest))
            weight = dot3(pair(self.gt, f), split(inner))
            if live is not None:
                weight = jnp.where(self.place < live(f), weight, 0.0)
            self.hold[c] = lead - weight
            if 2 * step < self.blocks:
                @pl.when(self.place % (4 * step) == step)
                def _():
                    self.lead_copy(c, self.place + step).start()

                @pl.when(self.place % (4 * step) == 3 * step)
                def _():
                    self.rest_copy(c, self.place - step).start()
            else:
                self.at_root(c)
            self.fin[c] = rest - dot3(split(self.nvec[f, 0]), split(weight))

    def climb(self, live, ahead=None, units=0):
        @pl.loop(0, max(self.chunks + self.levels - 1, units))
        def _(i):
            @pl.when(i < self.chunks)
            def _():
                self.leaf(i, live)

            for level in range(1, self.levels):
                @pl.when((i >= level) & (i < self.chunks + level))
                def _():
                    self.node(level, i - level, live)

            if ahead is not None:
                @pl.when(i < units)
                def _():
                    ahead(i)

    def finish(self, c, home_rows):
        f = c % self.fronts

        @pl.when(self.place == 0)
        def _():
            self.home_copy(c, home_rows).wait_recv()
            self.fin[c, pl.ds(0, home_rows)] = self.rest_in[c, pl.ds(0, home_rows)]
            if home_rows < self.width:
                self.fin[c, pl.ds(home_rows, self.width - home_rows)] = jnp.zeros(
                    (self.width - home_rows, self.chunk), F32)

        @pl.when(self.odd)
        def _():
            self.back_copy(c, self.place).wait_recv()
            self.fin[c] = self.top[c] - dot3(split(self.nvec[f, 0]), split(self.wrecv[c]))

    def result_copies(self, out, c):
        f, h = c % self.fronts, c // self.fronts
        columns = pl.ds(pl.multiple_of(h * self.chunk, self.chunk), self.chunk)
        w, rows = self.width, self.x.shape[1]
        return (
            pltpu.make_async_copy(self.body.at[c], out.at[f, pl.ds(w, rows - w), columns], self.fs.at[0, c]),
            pltpu.make_async_copy(self.fin.at[c], out.at[f, pl.ds(0, w), columns], self.fs.at[1, c]),
        )

    def drain(self, out, home_rows):
        root = self.blocks // 2

        @pl.when(self.odd)
        def _():
            for f in range(self.x.shape[0]):
                self.factor_copy(f, self.place).wait_send()

        @pl.loop(0, self.chunks)
        def _(c):
            @pl.when(self.odd)
            def _():
                self.up_copy(c, self.place).wait_send()

            @pl.when(~self.odd)
            def _():
                self.back_copy(c, self.place).wait_send()

            @pl.when(self.place % 4 == 0)
            def _():
                self.top_copy(c, self.place).wait_send()

            @pl.when((~self.odd) & (self.place != 0) & (self.place != root))
            def _():
                self.lead_copy(c, self.place).wait_send()

            @pl.when(self.place == root)
            def _():
                self.home_copy(c, home_rows).wait_send()

            for copy in self.result_copies(out, c):
                copy.wait()


def front_scratch(fronts, rows, cols, width, chunk):
    chunks = fronts * (cols // chunk)
    dma = pltpu.SemaphoreType.DMA
    piece = pltpu.VMEM((chunks, width, chunk), F32)
    return (
        [piece, pltpu.VMEM((chunks, rows - width, chunk), F32)]
        + [piece] * 9
        + [pltpu.VMEM((fronts, width, width), F32), pltpu.VMEM((2, fronts, width, rows), BF16)]
        + [pltpu.VMEM((2, fronts, width, width), BF16)] * 4
        + [dma((chunks,))] * 8
        + [dma((fronts,))] * 2
        + [dma((2, chunks))]
    )


def kernel(blocks, columns, rows_ref, live_ref, parent_ref, owner_ref, lx, lv, lf, mv, mf, ux, uv, uf, sv, sf, out_low, out_up, *s):
    place, column = lax.axis_index("rows"), lax.axis_index("fronts")
    vlx, vlv, vlf, vmv, vmf, vux, vuv, vuf, vsv, vsf, portions, tmat, load_sem, part_s, part_r, over_s, over_r = s[:17]
    low = Front(blocks, vlx, vlv, vlf, vmv, vmf, mf, LOW_CHUNK, s[17:45])
    up = Front(blocks, vux, vuv, vuf, vsv, vsf, sf, UP_CHUNK, s[45:73])
    fronts = lx.shape[0]
    share = portions.shape[3]
    root = blocks // 2

    pairs = []
    for f in range(fronts):
        pairs += [(lx.at[f], vlx.at[f]), (lv.at[f], vlv.at[f]), (lf.at[f], vlf.at[f]), (mv.at[f], vmv.at[f])]
    first = len(pairs)
    pairs += [(mf, vmf), (ux, vux), (uv, vuv), (uf, vuf), (sv, vsv), (sf, vsf)]
    loads = [pltpu.make_async_copy(a, b, load_sem.at[i]) for i, (a, b) in enumerate(pairs)]
    for copy in loads:
        copy.start()

    barrier = pltpu.get_barrier_semaphore()
    for shift in range(1, blocks):
        pl.semaphore_signal(barrier, inc=1, device_id={"rows": (place + shift) % blocks},
                            device_id_type=pl.DeviceIdType.MESH)
    for shift in range(1, columns):
        pl.semaphore_signal(barrier, inc=1, device_id={"fronts": (column + shift) % columns},
                            device_id_type=pl.DeviceIdType.MESH)
    pl.semaphore_wait(barrier, blocks + columns - 2)
    low.send_factors()

    def live(f):
        return live_ref[column * fronts + f]

    for f in range(fronts):
        for copy in loads[4 * f:4 * f + 4]:
            copy.wait()
        low.turn(f)
        low.tops(f, live)
        low.send_up(f)

    @pl.loop(fronts, low.chunks)
    def _(c):
        low.tops(c, live)
        low.send_up(c)

    up.send_factors()

    @pl.loop(0, low.chunks)
    def _(c):
        low.bodies(c)
        low.result_copies(out_low, c)[0].start()

    for copy in loads[first:]:
        copy.wait()
    low.turn_nodes()

    height, total = vux.shape[1], rows_ref.shape[0]
    lanes = rows_ref.shape[1]
    spots = total * share
    mine = jnp.broadcast_to(rows_ref[...].astype(F32)[:, None, :], (total, share, lanes)).reshape(spots, lanes)
    spot = lax.broadcasted_iota(jnp.int32, (spots, lanes), 0)
    lane = lax.broadcasted_iota(jnp.int32, (spots, lanes), 1)
    child = spot // share
    here_too = jnp.zeros((spots, lanes), F32)
    for c in range(total):
        owned = jnp.where(owner_ref[parent_ref[c]] == column, 1.0, 0.0)
        here_too = jnp.where(child == c, owned, here_too)
    wanted = (lane == place * share + spot % share) & (here_too > 0.0)
    base = (place * height).astype(F32)
    offset = jnp.sum(jnp.where(wanted, mine - base + 1.0, 0.0), axis=1, keepdims=True) - 1.0
    here = jnp.broadcast_to(offset, (spots, spots)).T[0:1]
    hit = lax.broadcasted_iota(jnp.int32, (height, spots), 0).astype(F32) == here
    chosen = jnp.where(hit, 1.0, 0.0)
    taken = jnp.sum(chosen, axis=1, keepdims=True) > 0.0
    up.turn(0)
    up.turn_nodes()
    one = chosen.astype(BF16)
    gram = jnp.dot(up.yt[0, 0], one, preferred_element_type=F32) + jnp.dot(
        up.yt[1, 0], one, preferred_element_type=F32)
    inner = split(dot3(pair(up.ft, 0), split(gram)))
    tmat[...] = chosen - dot3(split(vuv[0]), inner)
    vux[0] = jnp.where(taken, 0.0, vux[0])

    def ahead(c):
        up.tops(c, None)
        up.bodies(c)

    low.wait_factors()

    def part(c, r, peer):
        f, h = c % fronts, c // fronts
        return low.remote(
            low.hold.at[c, pl.ds(NPIV + r * share, share)], portions.at[column, f, h],
            part_s.at[r, c], part_r.at[c], peer)

    def over(c, shift, peer, slot):
        f, h = c % fronts, c // fronts
        return pltpu.make_async_remote_copy(
            portions.at[slot, f, h], portions.at[slot, f, h], over_s.at[shift, c], over_r.at[shift, c],
            device_id={"fronts": peer}, device_id_type=pl.DeviceIdType.MESH)

    def spread(c):
        for r in range(blocks):
            if r != root:
                part(c, r, r).start()
        portions[column, c % fronts, c // fronts] = low.hold[c, pl.ds(NPIV + root * share, share)]

    low.at_root = spread
    up.at_root = lambda c: up.home_copy(c, up.width).start()

    low.climb(live, ahead, up.chunks)

    @pl.loop(0, low.chunks)
    def _(c):
        @pl.when(place != root)
        def _():
            part(c, 0, place).wait_recv()

        for shift in range(1, columns):
            over(c, shift, (column + shift) % columns, column).start()

    @pl.when(place == root)
    def _():
        @pl.loop(0, low.chunks)
        def _(c):
            low.home_copy(c, NPIV).start()

    up.wait_factors()
    inside = LOW_CHUNK // UP_CHUNK

    for h in range(low.halves):
        for f in range(fronts):
            for shift in range(1, columns):
                over(h * fronts + f, shift, column, (column - shift + columns) % columns).wait_recv()
        arrived = split(portions[:, :, h].reshape(spots, LOW_CHUNK))
        gained = dot3(split(tmat[pl.ds(0, up.width)]), arrived)
        for k in range(inside):
            c = h * inside + k
            up.top[c] += gained[:, k * UP_CHUNK:(k + 1) * UP_CHUNK]
            up.send_up(c)

    @pl.loop(0, up.chunks)
    def _(c):
        h, k = c // inside, c % inside
        arrived = split(portions[:, :, h, :, pl.ds(pl.multiple_of(k * UP_CHUNK, UP_CHUNK), UP_CHUNK)].reshape(spots, UP_CHUNK))
        up.body[c] += dot3(split(tmat[pl.ds(up.width, height - up.width)]), arrived)
        up.result_copies(out_up, c)[0].start()

    up.climb(None)

    @pl.loop(0, low.chunks)
    def _(c):
        low.finish(c, NPIV)
        low.result_copies(out_low, c)[1].start()

    @pl.loop(0, up.chunks)
    def _(c):
        up.finish(c, up.width)
        up.result_copies(out_up, c)[1].start()

    @pl.when(place == root)
    def _():
        @pl.loop(0, low.chunks)
        def _(c):
            for r in range(blocks):
                if r != root:
                    part(c, r, r).wait_send()

    @pl.loop(0, low.chunks)
    def _(c):
        for shift in range(1, columns):
            over(c, shift, column, column).wait_send()

    low.drain(out_low, NPIV)
    up.drain(out_up, up.width)


def per_device(
    lower_rhs,
    lower_vectors,
    lower_factors,
    merge_vectors,
    merge_factors,
    live_blocks,
    parent_front,
    front_owner,
    contrib_rows,
    upper_rhs,
    upper_vectors,
    upper_factors,
    summit_vectors,
    summit_factors,
):
    blocks = lax.axis_size("rows")
    columns = lax.axis_size("fronts")
    fronts, height, cols = lower_rhs.shape
    width = lower_factors.shape[-1]
    share = (width - NPIV) // blocks
    dma = pltpu.SemaphoreType.DMA
    chunks = fronts * (cols // LOW_CHUNK)
    held = [lower_rhs, lower_vectors, lower_factors, merge_vectors, merge_factors]
    held += [upper_rhs, upper_vectors, upper_factors, summit_vectors, summit_factors]
    scratch = [pltpu.VMEM(a.shape, F32) for a in held]
    scratch += [
        pltpu.VMEM((columns, fronts, cols // LOW_CHUNK, share, LOW_CHUNK), F32),
        pltpu.VMEM((height, contrib_rows.shape[0] * share), F32),
        dma((4 * fronts + 6,)),
        dma((blocks, chunks)), dma((chunks,)), dma((columns, chunks)), dma((columns, chunks)),
    ]
    scratch += front_scratch(fronts, height, cols, width, LOW_CHUNK)
    scratch += front_scratch(upper_rhs.shape[0], height, cols, width, UP_CHUNK)
    anywhere = pl.BlockSpec(memory_space=pl.ANY)
    return pl.pallas_call(
        functools.partial(kernel, blocks, columns),
        out_shape=(
            jax.ShapeDtypeStruct(lower_rhs.shape, F32),
            jax.ShapeDtypeStruct(upper_rhs.shape, F32),
        ),
        in_specs=[pl.BlockSpec(memory_space=pltpu.VMEM)] + [pl.BlockSpec(memory_space=pltpu.SMEM)] * 3 + [anywhere] * 10,
        out_specs=(anywhere, anywhere),
        scratch_shapes=scratch,
        compiler_params=pltpu.CompilerParams(
            collective_id=0, has_side_effects=True, vmem_limit_bytes=56 * 1024 * 1024),
        name="two_level",
    )(contrib_rows, live_blocks, parent_front.reshape(-1), front_owner, lower_rhs, lower_vectors, lower_factors, merge_vectors, merge_factors,
      upper_rhs, upper_vectors, upper_factors, summit_vectors, summit_factors)


def solution(mesh):
    placed = (
        P("fronts", "rows", None),
        P("fronts", "rows", None),
        P("fronts", "rows", None, None),
        P("fronts", "rows", None, None),
        P("fronts", "rows", None, None),
        P(),
        P(),
        P(),
        P(),
        P("fronts", "rows", None),
        P("fronts", "rows", None),
        P("fronts", "rows", None, None),
        P("fronts", "rows", None, None),
        P("fronts", "rows", None, None),
    )
    return jax.shard_map(
        per_device,
        mesh=mesh,
        in_specs=placed,
        out_specs=(P("fronts", "rows", None), P("fronts", "rows", None)),
        check_vma=False,
    )
```

```python
import functools

import jax
import jax.numpy as jnp
from jax import lax
from jax.experimental import pallas as pl
from jax.experimental.pallas import tpu as pltpu
from jax.sharding import PartitionSpec as P

NPIV = 128
LOW_CHUNK = 128
UP_CHUNK = 128
F32 = jnp.float32
BF16 = jnp.bfloat16


def split(x):
    high = x.astype(BF16)
    return high, (x - high.astype(F32)).astype(BF16)


def pair(ref, f):
    return ref[0, f], ref[1, f]


def dot3(a, b):
    (ah, al), (bh, bl) = a, b
    one = functools.partial(jnp.dot, preferred_element_type=F32)
    return one(ah, bh) + (one(ah, bl) + one(al, bh))


class Front:
    def __init__(self, blocks, x, vec, fac, nvec, nfac, nfac_any, chunk, s):
        self.blocks, self.levels, self.chunk = blocks, blocks.bit_length() - 1, chunk
        self.x, self.vec, self.fac, self.nvec, self.nfac, self.nfac_any = x, vec, fac, nvec, nfac, nfac_any
        (self.top, self.body, self.usend, self.urecv, self.wsend, self.wrecv, self.fin, self.hold,
         self.lead_in, self.rest_in, self.scaled, self.first,
         self.yt, self.vt, self.gt, self.ft, self.first_t,
         self.us, self.ur, self.ws, self.wr, self.ts, self.hs, self.li, self.ri,
         self.gs, self.gr, self.fs) = s
        self.halves = x.shape[2] // chunk
        self.fronts = x.shape[0]
        self.chunks = self.fronts * self.halves
        self.width = fac.shape[-1]
        self.place = lax.axis_index("rows")
        self.odd = self.place % 2 == 1

    def remote(self, src, dst, send, recv, peer):
        return pltpu.make_async_remote_copy(
            src, dst, send, recv, device_id={"rows": peer}, device_id_type=pl.DeviceIdType.MESH)

    def factor_copy(self, f, peer):
        return self.remote(self.nfac_any.at[f, 0], self.first.at[f], self.gs.at[f], self.gr.at[f], peer)

    def send_factors(self):
        @pl.when(self.odd)
        def _():
            for f in range(self.x.shape[0]):
                self.factor_copy(f, self.place - 1).start()

    def wait_factors(self):
        @pl.when(~self.odd)
        def _():
            for f in range(self.x.shape[0]):
                self.factor_copy(f, self.place).wait_recv()
                self.keep(self.first_t, f, self.first[f])

    def keep(self, ref, f, value):
        ref[0, f], ref[1, f] = split(value.T)

    def turn(self, f):
        self.keep(self.yt, f, self.vec[f])
        self.keep(self.ft, f, self.fac[f, 0])
        self.keep(self.vt, f, self.nvec[f, 0])

    def turn_nodes(self):
        for f in range(self.x.shape[0]):
            self.keep(self.gt, f, self.nfac[f, 0])

    def up_copy(self, c, peer):
        return self.remote(self.usend.at[c], self.urecv.at[c], self.us.at[c], self.ur.at[c], peer)

    def back_copy(self, c, peer):
        return self.remote(self.wsend.at[c], self.wrecv.at[c], self.ws.at[c], self.wr.at[c], peer)

    def top_copy(self, c, peer):
        return self.remote(self.top.at[c], self.lead_in.at[c], self.ts.at[c], self.li.at[c], peer)

    def lead_copy(self, c, peer):
        return self.remote(self.hold.at[c], self.lead_in.at[c], self.hs.at[c], self.li.at[c], peer)

    def rest_copy(self, c, peer):
        return self.remote(self.hold.at[c], self.rest_in.at[c], self.hs.at[c], self.ri.at[c], peer)

    def home_copy(self, c, rows):
        span = pl.ds(0, rows)
        return self.remote(self.hold.at[c, span], self.rest_in.at[c, span], self.hs.at[c], self.ri.at[c], 0)

    def tops(self, c, live):
        f, h = c % self.fronts, c // self.fronts
        columns = pl.ds(pl.multiple_of(h * self.chunk, self.chunk), self.chunk)
        x = self.x[f, :, columns]
        project = dot3(pair(self.yt, f), split(x))
        scaled = dot3(pair(self.ft, f), split(project))
        if live is not None:
            scaled = jnp.where(self.place < live(f), scaled, 0.0)
        self.scaled[c] = scaled
        w = self.width
        self.top[c] = x[:w] - dot3(split(self.vec[f, pl.ds(0, w)]), split(scaled))

    def send_up(self, c):
        f = c % self.fronts

        @pl.when(self.odd)
        def _():
            self.usend[c] = dot3(pair(self.vt, f), split(self.top[c]))
            self.up_copy(c, self.place - 1).start()

    def bodies(self, c):
        f, h = c % self.fronts, c // self.fronts
        columns = pl.ds(pl.multiple_of(h * self.chunk, self.chunk), self.chunk)
        w = self.width
        lower = pl.ds(w, self.x.shape[1] - w)
        self.body[c] = self.x[f, lower, columns] - dot3(split(self.vec[f, lower]), split(self.scaled[c]))

    def leaf(self, c, live):
        @pl.when(~self.odd)
        def _():
            f = c % self.fronts
            peer = self.place + 1
            self.up_copy(c, peer).wait_recv()
            top = self.top[c]
            weight = dot3(pair(self.first_t, f), split(top + self.urecv[c]))
            if live is not None:
                weight = jnp.where(peer < live(f), weight, 0.0)
            self.top[c] = top - weight

            @pl.when(self.place % 4 == 0)
            def _():
                self.top_copy(c, self.place + 2).start()

            self.wsend[c] = weight
            self.back_copy(c, peer).start()

    def node(self, level, c, live):
        step = 1 << level

        @pl.when(self.place % (2 * step) == step)
        def _():
            f = c % self.fronts
            self.lead_copy(c, self.place).wait_recv()
            if level > 1:
                self.rest_copy(c, self.place).wait_recv()
            rest = self.top[c] if level == 1 else self.rest_in[c]
            lead = self.lead_in[c]
            inner = lead + dot3(pair(self.vt, f), split(rest))
            weight = dot3(pair(self.gt, f), split(inner))
            if live is not None:
                weight = jnp.where(self.place < live(f), weight, 0.0)
            self.hold[c] = lead - weight
            if 2 * step < self.blocks:
                @pl.when(self.place % (4 * step) == step)
                def _():
                    self.lead_copy(c, self.place + step).start()

                @pl.when(self.place % (4 * step) == 3 * step)
                def _():
                    self.rest_copy(c, self.place - step).start()
            else:
                self.at_root(c)
            self.fin[c] = rest - dot3(split(self.nvec[f, 0]), split(weight))

    def climb(self, live, ahead=None, units=0):
        @pl.loop(0, max(self.chunks + self.levels - 1, units))
        def _(i):
            @pl.when(i < self.chunks)
            def _():
                self.leaf(i, live)

            for level in range(1, self.levels):
                @pl.when((i >= level) & (i < self.chunks + level))
                def _():
                    self.node(level, i - level, live)

            if ahead is not None:
                @pl.when(i < units)
                def _():
                    ahead(i)

    def finish(self, c, home_rows):
        f = c % self.fronts

        @pl.when(self.place == 0)
        def _():
            self.home_copy(c, home_rows).wait_recv()
            self.fin[c, pl.ds(0, home_rows)] = self.rest_in[c, pl.ds(0, home_rows)]
            if home_rows < self.width:
                self.fin[c, pl.ds(home_rows, self.width - home_rows)] = jnp.zeros(
                    (self.width - home_rows, self.chunk), F32)

        @pl.when(self.odd)
        def _():
            self.back_copy(c, self.place).wait_recv()
            self.fin[c] = self.top[c] - dot3(split(self.nvec[f, 0]), split(self.wrecv[c]))

    def result_copies(self, out, c):
        f, h = c % self.fronts, c // self.fronts
        columns = pl.ds(pl.multiple_of(h * self.chunk, self.chunk), self.chunk)
        w, rows = self.width, self.x.shape[1]
        return (
            pltpu.make_async_copy(self.body.at[c], out.at[f, pl.ds(w, rows - w), columns], self.fs.at[0, c]),
            pltpu.make_async_copy(self.fin.at[c], out.at[f, pl.ds(0, w), columns], self.fs.at[1, c]),
        )

    def drain(self, out, home_rows):
        root = self.blocks // 2

        @pl.when(self.odd)
        def _():
            for f in range(self.x.shape[0]):
                self.factor_copy(f, self.place).wait_send()

        @pl.loop(0, self.chunks)
        def _(c):
            @pl.when(self.odd)
            def _():
                self.up_copy(c, self.place).wait_send()

            @pl.when(~self.odd)
            def _():
                self.back_copy(c, self.place).wait_send()

            @pl.when(self.place % 4 == 0)
            def _():
                self.top_copy(c, self.place).wait_send()

            @pl.when((~self.odd) & (self.place != 0) & (self.place != root))
            def _():
                self.lead_copy(c, self.place).wait_send()

            @pl.when(self.place == root)
            def _():
                self.home_copy(c, home_rows).wait_send()

            for copy in self.result_copies(out, c):
                copy.wait()


def front_scratch(fronts, rows, cols, width, chunk):
    chunks = fronts * (cols // chunk)
    dma = pltpu.SemaphoreType.DMA
    piece = pltpu.VMEM((chunks, width, chunk), F32)
    return (
        [piece, pltpu.VMEM((chunks, rows - width, chunk), F32)]
        + [piece] * 9
        + [pltpu.VMEM((fronts, width, width), F32), pltpu.VMEM((2, fronts, width, rows), BF16)]
        + [pltpu.VMEM((2, fronts, width, width), BF16)] * 4
        + [dma((chunks,))] * 8
        + [dma((fronts,))] * 2
        + [dma((2, chunks))]
    )


def kernel(blocks, columns, rows_ref, live_ref, parent_ref, owner_ref, lx, lv, lf, mv, mf, ux, uv, uf, sv, sf, out_low, out_up, *s):
    place, column = lax.axis_index("rows"), lax.axis_index("fronts")
    vlx, vlv, vlf, vmv, vmf, vux, vuv, vuf, vsv, vsf, portions, tmat, load_sem, part_s, part_r, over_s, over_r = s[:17]
    low = Front(blocks, vlx, vlv, vlf, vmv, vmf, mf, LOW_CHUNK, s[17:45])
    up = Front(blocks, vux, vuv, vuf, vsv, vsf, sf, UP_CHUNK, s[45:73])
    fronts = lx.shape[0]
    share = portions.shape[3]
    root = blocks // 2

    pairs = []
    for f in range(fronts):
        pairs += [(lx.at[f], vlx.at[f]), (lv.at[f], vlv.at[f]), (lf.at[f], vlf.at[f]), (mv.at[f], vmv.at[f])]
    first = len(pairs)
    pairs += [(mf, vmf), (ux, vux), (uv, vuv), (uf, vuf), (sv, vsv), (sf, vsf)]
    loads = [pltpu.make_async_copy(a, b, load_sem.at[i]) for i, (a, b) in enumerate(pairs)]
    for copy in loads:
        copy.start()

    barrier = pltpu.get_barrier_semaphore()
    for shift in range(1, blocks):
        pl.semaphore_signal(barrier, inc=1, device_id={"rows": (place + shift) % blocks},
                            device_id_type=pl.DeviceIdType.MESH)
    for shift in range(1, columns):
        pl.semaphore_signal(barrier, inc=1, device_id={"fronts": (column + shift) % columns},
                            device_id_type=pl.DeviceIdType.MESH)
    pl.semaphore_wait(barrier, blocks + columns - 2)
    low.send_factors()

    def live(f):
        return live_ref[column * fronts + f]

    for f in range(fronts):
        for copy in loads[4 * f:4 * f + 4]:
            copy.wait()
        low.turn(f)
        low.tops(f, live)
        low.send_up(f)

    @pl.loop(fronts, low.chunks)
    def _(c):
        low.tops(c, live)
        low.send_up(c)

    up.send_factors()

    @pl.loop(0, low.chunks)
    def _(c):
        low.bodies(c)
        low.result_copies(out_low, c)[0].start()

    for copy in loads[first:]:
        copy.wait()
    low.turn_nodes()

    height, total = vux.shape[1], rows_ref.shape[0]
    lanes = rows_ref.shape[1]
    spots = total * share
    mine = jnp.broadcast_to(rows_ref[...].astype(F32)[:, None, :], (total, share, lanes)).reshape(spots, lanes)
    spot = lax.broadcasted_iota(jnp.int32, (spots, lanes), 0)
    lane = lax.broadcasted_iota(jnp.int32, (spots, lanes), 1)
    child = spot // share
    here_too = jnp.zeros((spots, lanes), F32)
    for c in range(total):
        owned = jnp.where(owner_ref[parent_ref[c]] == column, 1.0, 0.0)
        here_too = jnp.where(child == c, owned, here_too)
    wanted = (lane == place * share + spot % share) & (here_too > 0.0)
    base = (place * height).astype(F32)
    offset = jnp.sum(jnp.where(wanted, mine - base + 1.0, 0.0), axis=1, keepdims=True) - 1.0
    here = jnp.broadcast_to(offset, (spots, spots)).T[0:1]
    hit = lax.broadcasted_iota(jnp.int32, (height, spots), 0).astype(F32) == here
    chosen = jnp.where(hit, 1.0, 0.0)
    taken = jnp.sum(chosen, axis=1, keepdims=True) > 0.0
    up.turn(0)
    up.turn_nodes()
    one = chosen.astype(BF16)
    gram = jnp.dot(up.yt[0, 0], one, preferred_element_type=F32) + jnp.dot(
        up.yt[1, 0], one, preferred_element_type=F32)
    inner = split(dot3(pair(up.ft, 0), split(gram)))
    tmat[...] = chosen - dot3(split(vuv[0]), inner)
    vux[0] = jnp.where(taken, 0.0, vux[0])

    def ahead(c):
        up.tops(c, None)
        up.bodies(c)

    low.wait_factors()

    def part(c, r, peer):
        f, h = c % fronts, c // fronts
        return low.remote(
            low.hold.at[c, pl.ds(NPIV + r * share, share)], portions.at[column, f, h],
            part_s.at[r, c], part_r.at[c], peer)

    def over(c, shift, peer, slot):
        f, h = c % fronts, c // fronts
        return pltpu.make_async_remote_copy(
            portions.at[slot, f, h], portions.at[slot, f, h], over_s.at[shift, c], over_r.at[shift, c],
            device_id={"fronts": peer}, device_id_type=pl.DeviceIdType.MESH)

    def spread(c):
        for r in range(blocks):
            if r != root:
                part(c, r, r).start()
        portions[column, c % fronts, c // fronts] = low.hold[c, pl.ds(NPIV + root * share, share)]

    low.at_root = spread
    up.at_root = lambda c: up.home_copy(c, up.width).start()

    low.climb(live, ahead, up.chunks)

    @pl.loop(0, low.chunks)
    def _(c):
        @pl.when(place != root)
        def _():
            part(c, 0, place).wait_recv()

        for shift in range(1, columns):
            over(c, shift, (column + shift) % columns, column).start()

    @pl.when(place == root)
    def _():
        @pl.loop(0, low.chunks)
        def _(c):
            low.home_copy(c, NPIV).start()

    up.wait_factors()
    inside = LOW_CHUNK // UP_CHUNK

    for h in range(low.halves):
        for f in range(fronts):
            for shift in range(1, columns):
                over(h * fronts + f, shift, column, (column - shift + columns) % columns).wait_recv()
        arrived = split(portions[:, :, h].reshape(spots, LOW_CHUNK))
        gained = dot3(split(tmat[pl.ds(0, up.width)]), arrived)
        for k in range(inside):
            c = h * inside + k
            up.top[c] += gained[:, k * UP_CHUNK:(k + 1) * UP_CHUNK]
            up.send_up(c)

    @pl.loop(0, up.chunks)
    def _(c):
        h, k = c // inside, c % inside
        arrived = split(portions[:, :, h, :, pl.ds(pl.multiple_of(k * UP_CHUNK, UP_CHUNK), UP_CHUNK)].reshape(spots, UP_CHUNK))
        up.body[c] += dot3(split(tmat[pl.ds(up.width, height - up.width)]), arrived)
        up.result_copies(out_up, c)[0].start()

    up.climb(None)

    @pl.loop(0, low.chunks)
    def _(c):
        low.finish(c, NPIV)
        low.result_copies(out_low, c)[1].start()

    @pl.loop(0, up.chunks)
    def _(c):
        up.finish(c, up.width)
        up.result_copies(out_up, c)[1].start()

    @pl.when(place == root)
    def _():
        @pl.loop(0, low.chunks)
        def _(c):
            for r in range(blocks):
                if r != root:
                    part(c, r, r).wait_send()

    @pl.loop(0, low.chunks)
    def _(c):
        for shift in range(1, columns):
            over(c, shift, column, column).wait_send()

    low.drain(out_low, NPIV)
    up.drain(out_up, up.width)


def per_device(
    lower_rhs,
    lower_vectors,
    lower_factors,
    merge_vectors,
    merge_factors,
    live_blocks,
    parent_front,
    front_owner,
    contrib_rows,
    upper_rhs,
    upper_vectors,
    upper_factors,
    summit_vectors,
    summit_factors,
):
    blocks = lax.axis_size("rows")
    columns = lax.axis_size("fronts")
    fronts, height, cols = lower_rhs.shape
    width = lower_factors.shape[-1]
    share = (width - NPIV) // blocks
    dma = pltpu.SemaphoreType.DMA
    chunks = fronts * (cols // LOW_CHUNK)
    held = [lower_rhs, lower_vectors, lower_factors, merge_vectors, merge_factors]
    held += [upper_rhs, upper_vectors, upper_factors, summit_vectors, summit_factors]
    scratch = [pltpu.VMEM(a.shape, F32) for a in held]
    scratch += [
        pltpu.VMEM((columns, fronts, cols // LOW_CHUNK, share, LOW_CHUNK), F32),
        pltpu.VMEM((height, contrib_rows.shape[0] * share), F32),
        dma((4 * fronts + 6,)),
        dma((blocks, chunks)), dma((chunks,)), dma((columns, chunks)), dma((columns, chunks)),
    ]
    scratch += front_scratch(fronts, height, cols, width, LOW_CHUNK)
    scratch += front_scratch(upper_rhs.shape[0], height, cols, width, UP_CHUNK)
    anywhere = pl.BlockSpec(memory_space=pl.ANY)
    return pl.pallas_call(
        functools.partial(kernel, blocks, columns),
        out_shape=(
            jax.ShapeDtypeStruct(lower_rhs.shape, F32),
            jax.ShapeDtypeStruct(upper_rhs.shape, F32),
        ),
        in_specs=[pl.BlockSpec(memory_space=pltpu.VMEM)] + [pl.BlockSpec(memory_space=pltpu.SMEM)] * 3 + [anywhere] * 10,
        out_specs=(anywhere, anywhere),
        scratch_shapes=scratch,
        compiler_params=pltpu.CompilerParams(
            collective_id=0, has_side_effects=True, vmem_limit_bytes=56 * 1024 * 1024),
        name="two_level",
    )(contrib_rows, live_blocks, parent_front.reshape(-1), front_owner, lower_rhs, lower_vectors, lower_factors, merge_vectors, merge_factors,
      upper_rhs, upper_vectors, upper_factors, summit_vectors, summit_factors)


def solution(mesh):
    placed = (
        P("fronts", "rows", None),
        P("fronts", "rows", None),
        P("fronts", "rows", None, None),
        P("fronts", "rows", None, None),
        P("fronts", "rows", None, None),
        P(),
        P(),
        P(),
        P(),
        P("fronts", "rows", None),
        P("fronts", "rows", None),
        P("fronts", "rows", None, None),
        P("fronts", "rows", None, None),
        P("fronts", "rows", None, None),
    )
    return jax.shard_map(
        per_device,
        mesh=mesh,
        in_specs=placed,
        out_specs=(P("fronts", "rows", None), P("fronts", "rows", None)),
        check_vma=False,
    )
```
